32 devices in a mesh: seq: 8 (over z, y), head: 4 (over x, core).
Axes of the slice: x: 2, y: 2, z: 4, core: 2. Of those that a mesh axis runs over, the one named last changes fastest.
Arguments:
- inner_input: bfloat16 [2048, 8192], P('seq', 'head'), may hold values from -6 to 6
- state_input: bfloat16 [2048, 2, 1024], P('seq', None, 'head'), may hold values from -3 to 3
- gate_input: bfloat16 [2048, 8192], P('seq', 'head'), may hold values from -6 to 6
- step_input: float32 [128, 2048], P('head', 'seq'), may hold values from -4.7 to 0.6
- decay_exponent: float32 [128], P('head')
- skip_gain: float32 [128], P('head'), may hold values from 0.5 to 1.5
- documents: int32 [2048], P('seq'), may hold values from 0 to 1, never falling along the last dimension, each value on 1 to 1536 neighbouring positions
- filter_inner: float32 [4, 8192], P(None, 'head'), may hold values from -3 to 3
- filter_state: float32 [4, 2, 1024], P(None, None, 'head'), may hold values from -3 to 3
- norm_gain: float32 [8192], P('head'), may hold values from 0.1 to 1.9
- output_weight: bfloat16 [8192, 4096], P('head', 'seq'), may hold values from -0.0625 to 0.0625
Outputs:
- mixed: bfloat16 [2048, 4096], P('seq', 'head')
The draws below stay inside these ranges and needn't reach their ends.
Inputs may be any that keep to these rules, and one draw needn't show every extreme that they name: `documents`: document numbers never fall along the sequence.
All inputs are finite; a program needn't handle non-finite values.
Results may differ from the reference program's by a relative error of at most 0.0058.
Values may be sent and summed in bfloat16 or wider, within the bound.
A program may use at most 192 MiB of HBM per device.

```python
import math
import jax
import jax.numpy as jnp
import numpy as np
from jax import lax

D = 4096
HEADS = 128
HEAD_DIM = 64
STATE = 128
GROUPS = 8
INNER = 8192
KERNEL = 4
SPAN = 256
TOK_DEV = 256
TOKENS = 2048
DOCS = 2
DOC_MOST = 1536


def head_split(key):
    chosen = jax.random.uniform(jax.random.fold_in(key, 101), (HEADS,))
    share = 0.5
    return chosen < share


def draw_step_input(key, part):
    slow = head_split(key)
    base_step = jnp.where(slow, 0.02, 0.5)
    roughness = jnp.exp(jax.random.uniform(jax.random.fold_in(key, 202), (HEADS, TOKENS), minval=-0.7, maxval=0.7))
    value = base_step[:, None] * roughness
    return jnp.log(jnp.expm1(value)).astype(jnp.float32)


def draw_decay_exponent(key, part):
    slow = head_split(key)
    position = jax.random.uniform(jax.random.fold_in(key, 303), (HEADS,))
    slow_rate = 0.3 * jnp.power(5.0, position) / (6.0 * TOK_DEV)
    fast_rate = 0.02 * jnp.power(2.0, position)
    base_step = jnp.where(slow, 0.02, 0.5)
    chosen_rate = jnp.where(slow, slow_rate, fast_rate)
    return jnp.log(chosen_rate / base_step).astype(jnp.float32)


def level_of(key, dims, shards, low, high):
    def one(dim, shards_of):
        steps = jax.random.uniform(jax.random.fold_in(jax.random.fold_in(key, 6), dim), (shards_of,), jnp.float32, low / len(shards), high / len(shards))
        return jnp.repeat(jnp.exp(steps), dims[dim] // shards_of).reshape((-1,) + (1,) * (len(dims) - dim - 1))

    level = one(*shards[0])
    for cut in shards[1:]:
        level = level * one(*cut)
    return level


def split_up(count, total, most, lean):
    portions = [(1 << 20) // math.isqrt(rank ** lean) + 1 for rank in range(2, count + 1)]
    surplus, holding = total - most - (count - 1), [1] * (count - 1)
    while surplus > 0:
        movable = [i for i in range(count - 1) if holding[i] < most]
        whole, remaining = sum([portions[i] for i in movable]), surplus
        for i in movable:
            addition = min(most - holding[i], max(1, remaining * portions[i] // whole), surplus)
            holding[i] = holding[i] + addition
            surplus = surplus - addition
    return np.array([most] + holding)


def ragged(stream_key, amount, total, limit, lean):
    if amount == 2:
        one = jax.random.randint(stream_key, (), max(1, total - limit), min(limit, total - 1) + 1)
        return jnp.stack([one, total - one])
    lengths = jnp.asarray(split_up(amount, total, limit, lean), jnp.int32)
    couples = (amount - 1) // 2
    source_of, receiver = lengths[1:1 + 2 * couples:2], lengths[2:2 + 2 * couples:2]
    room = jnp.minimum(source_of - 1, limit - receiver)
    shifted = jax.random.randint(jax.random.fold_in(stream_key, 1), (couples,), 0, 1 << 20) % (room + 1)
    lengths = lengths.at[1:1 + 2 * couples:2].set(source_of - shifted).at[2:2 + 2 * couples:2].set(receiver + shifted)
    return lengths[jax.random.permutation(jax.random.fold_in(stream_key, 2), amount)]


def bell_draw(rng, extent, scale, most, cuts=(), dtype=jnp.bfloat16):
    values = jax.random.normal(rng, extent, jnp.float32) * scale
    if len(cuts) > 0:
        values = level_of(rng, extent, cuts, -0.22, 0.18) * values
    return jnp.clip(values, min=-most, max=most).astype(dtype)


def setup_inputs(seed: int = 0) -> dict:
    streams_of = jax.random.split(jax.random.key(seed), 12)
    return {
        "inner_input": bell_draw(streams_of[0], (TOKENS, INNER), 1.0, 6.0, ((0, 8), (1, 4))),
        "state_input": bell_draw(streams_of[1], (TOKENS, 2, GROUPS * STATE), 0.5, 3.0, ((0, 8), (2, 4))),
        "gate_input": bell_draw(streams_of[2], (TOKENS, INNER), 1.0, 6.0, ((0, 8), (1, 4))),
        "step_input": draw_step_input(jax.random.fold_in(streams_of[11], 71), 0),
        "decay_exponent": draw_decay_exponent(jax.random.fold_in(streams_of[11], 71), 0),
        "skip_gain": jnp.clip(0.5 + 1.0 * jax.random.uniform(streams_of[5], (HEADS,), jnp.float32) ** level_of(streams_of[5], (HEADS,), ((0, 4),), -0.2, 0.2), 0.5, 1.5),
        "documents": jnp.searchsorted(jnp.cumsum(ragged(streams_of[6], DOCS, TOKENS, DOC_MOST, 1)), jnp.arange(TOKENS), side="right").astype(jnp.int32),
        "filter_inner": bell_draw(streams_of[7], (KERNEL, INNER), KERNEL ** -0.5, 3.0, ((1, 4),), jnp.float32),
        "filter_state": bell_draw(streams_of[8], (KERNEL, 2, GROUPS * STATE), KERNEL ** -0.5, 3.0, ((2, 4),), jnp.float32),
        "norm_gain": jnp.clip(1.0 + 0.18 * jax.random.normal(streams_of[9], (INNER,), jnp.float32), 0.1, 1.9),
        "output_weight": bell_draw(streams_of[10], (INNER, D), INNER ** -0.5, 0.0625, ((0, 4), (1, 8))),
    }


highest = lax.Precision.HIGHEST

def causal_conv(extended, weights, segments_wide, segment_block):
    length = segment_block.shape[0]
    running = jnp.zeros(extended[:length].shape, jnp.float32)
    for offset in range(KERNEL):
        window = extended[offset:offset + length].astype(jnp.float32)
        matches = segments_wide[offset:offset + length] == segment_block
        matches = matches.reshape((length,) + (1,) * (extended.ndim - 1))
        running = running + jnp.where(matches, window * weights[offset], jnp.float32(0.0))
    return jax.nn.silu(running).astype(jnp.bfloat16)

def span_parts(values, write_rows, read_rows, step_size, decay_rate, segment_block, prior_segment):
    length = segment_block.shape[0]
    repeat = decay_rate.shape[0] // write_rows.shape[1]
    cumulative = jnp.cumsum(decay_rate, axis=1)
    places = jnp.arange(length)
    linked = (segment_block[:, None] == segment_block[None, :]) & (places[:, None] >= places[None, :])
    spread = cumulative[:, :, None] - cumulative[:, None, :]
    decays = jnp.exp(jnp.where(linked[None], spread, -jnp.inf))
    scores = jnp.einsum('ign,jgn->gij', read_rows.astype(jnp.float32), write_rows.astype(jnp.float32), precision=highest)
    scores = jnp.repeat(scores, repeat, axis=0)
    mixing = lax.optimization_barrier((decays * scores * step_size[:, None, :]).astype(jnp.bfloat16))
    within = jnp.einsum('hij,jhp->ihp', mixing.astype(jnp.float32), values.astype(jnp.float32), precision=highest)
    inflow = jnp.exp(cumulative) * (segment_block == prior_segment)[None, :].astype(jnp.float32)
    final_segment = segment_block[-1]
    closing = jnp.exp(cumulative[:, -1:] - cumulative) * (segment_block == final_segment)[None, :].astype(jnp.float32) * step_size
    weighted = lax.optimization_barrier((values.astype(jnp.float32) * closing.T[:, :, None]).astype(jnp.bfloat16))
    writes = jnp.repeat(write_rows, repeat, axis=1).astype(jnp.float32)
    deposit = jnp.einsum('jhp,jhn->hpn', weighted.astype(jnp.float32), writes, precision=highest)
    fading = jnp.exp(cumulative[:, -1]) * (final_segment == prior_segment).astype(jnp.float32)
    return (within, inflow, fading, deposit)

def reading(read_rows, held_state, repeat):
    readers = jnp.repeat(read_rows, repeat, axis=1).astype(jnp.float32)
    return jnp.einsum('ihn,hpn->ihp', readers, held_state, precision=highest)

def gated_norm(outputs, gates, norm_scale):
    height = outputs.shape[0]
    gated = outputs * jax.nn.silu(gates.astype(jnp.float32))
    grouped = gated.reshape(height, -1, INNER // GROUPS)
    mean_square = lax.optimization_barrier(jnp.mean(grouped * grouped, axis=-1, keepdims=True))
    normed = (grouped * lax.rsqrt(mean_square + 1e-05)).reshape(height, -1) * norm_scale
    return normed.astype(jnp.bfloat16)

def reference(inner_input, state_input, gate_input, step_input, decay_exponent, skip_gain, documents, filter_inner, filter_state, norm_gain, output_weight):
    span_count = TOKENS // SPAN
    margin = KERNEL - 1
    repeat = HEADS // GROUPS
    inner_blocks = inner_input.reshape(span_count, SPAN, INNER)
    state_blocks = state_input.reshape(span_count, SPAN, 2, GROUPS * STATE)
    gate_blocks = gate_input.reshape(span_count, SPAN, INNER)
    raw_blocks = step_input.reshape(HEADS, span_count, SPAN).transpose(1, 0, 2)
    segment_blocks = documents.reshape(span_count, SPAN)

    def advance(carried, pieces):
        state_now, prior_inner, prior_state, prior_segments = carried
        inner_block, state_block, gate_block, raw_block, segment_block = pieces
        segments_wide = jnp.concatenate([prior_segments, segment_block])
        inner_conv = causal_conv(jnp.concatenate([prior_inner, inner_block]), filter_inner, segments_wide, segment_block)
        state_conv = causal_conv(jnp.concatenate([prior_state, state_block]), filter_state, segments_wide, segment_block)
        values = inner_conv.reshape(SPAN, HEADS, HEAD_DIM)
        write_rows = state_conv[:, 0].reshape(SPAN, GROUPS, STATE)
        read_rows = state_conv[:, 1].reshape(SPAN, GROUPS, STATE)
        step_size = jax.nn.softplus(raw_block)
        decay_rate = -step_size * jnp.exp(decay_exponent)[:, None]
        within, inflow, fading, deposit = span_parts(values, write_rows, read_rows, step_size, decay_rate, segment_block, prior_segments[-1])
        scan_out = within + inflow.T[:, :, None] * reading(read_rows, state_now, repeat) + skip_gain[None, :, None] * values.astype(jnp.float32)
        state_now = fading[:, None, None] * state_now + deposit
        normed = gated_norm(scan_out.reshape(SPAN, INNER), gate_block, norm_gain)
        mixed = jnp.dot(normed, output_weight, preferred_element_type=jnp.float32).astype(jnp.bfloat16)
        return ((state_now, inner_block[-margin:], state_block[-margin:], segment_block[-margin:]), mixed)
    initial = (jnp.zeros((HEADS, HEAD_DIM, STATE), jnp.float32), jnp.zeros((margin, INNER), jnp.bfloat16), jnp.zeros((margin, 2, GROUPS * STATE), jnp.bfloat16), jnp.full((margin,), -1, jnp.int32))
    _, mixed = lax.scan(advance, initial, (inner_blocks, state_blocks, gate_blocks, raw_blocks, segment_blocks))
    return mixed.reshape(TOKENS, D)
```

```python
import jax
import jax.numpy as jnp
from jax import lax
from jax.experimental import pallas as pl
from jax.experimental.pallas import tpu as pltpu
from jax.sharding import PartitionSpec as P

HEAD_DIM = 64
STATE = 128
GROUPS = 8
INNER = 8192
KERNEL = 4


highest = lax.Precision.HIGHEST


def entering(part, axis, combine, identity):
    place = lax.axis_index(axis)
    gathered = jax.tree.map(lambda a: lax.all_gather(a, axis), part)
    state = jax.tree.map(lambda a, e: jnp.zeros_like(a) + jnp.asarray(e, a.dtype), part, identity)

    def one(step, state):
        return combine(
            state, jax.tree.map(lambda a: lax.dynamic_index_in_dim(a, step, 0, False), gathered)
        )

    return lax.fori_loop(0, place, one, state)


def passed_along(value, axis, steps):
    count = lax.axis_size(axis)
    initial, last = (max(0, -steps), min(count, count - steps))
    return lax.ppermute(value, axis, [(source, source + steps) for source in range(initial, last)])


def causal_conv(extended, weights, segments_wide, segment_block):
    length = segment_block.shape[0]
    running = jnp.zeros(extended[:length].shape, jnp.float32)
    for offset in range(KERNEL):
        window = extended[offset : offset + length].astype(jnp.float32)
        matches = segments_wide[offset : offset + length] == segment_block
        matches = matches.reshape((length,) + (1,) * (extended.ndim - 1))
        running = running + jnp.where(matches, window * weights[offset], jnp.float32(0.0))
    return jax.nn.silu(running).astype(jnp.bfloat16)


def span_parts(values, write_rows, read_rows, step_size, decay_rate, segment_block, prior_segment):
    length = segment_block.shape[0]
    repeat = decay_rate.shape[0] // write_rows.shape[1]
    cumulative = jnp.cumsum(decay_rate, axis=1)
    places = jnp.arange(length)
    linked = (segment_block[:, None] == segment_block[None, :]) & (
        places[:, None] >= places[None, :]
    )
    spread = cumulative[:, :, None] - cumulative[:, None, :]
    decays = jnp.exp(jnp.where(linked[None], spread, -jnp.inf))
    scores = jnp.einsum("ign,jgn->gij", read_rows, write_rows, preferred_element_type=jnp.float32)
    scores = jnp.repeat(scores, repeat, axis=0)
    mixing = (decays * scores * step_size[:, None, :]).astype(jnp.bfloat16)
    within = jnp.einsum("hij,jhp->ihp", mixing, values, preferred_element_type=jnp.float32)
    inflow = jnp.exp(cumulative) * (segment_block == prior_segment)[None, :].astype(jnp.float32)
    final_segment = segment_block[-1]
    closing = (
        jnp.exp(cumulative[:, -1:] - cumulative)
        * (segment_block == final_segment)[None, :].astype(jnp.float32)
        * step_size
    )
    weighted = (values.astype(jnp.float32) * closing.T[:, :, None]).astype(jnp.bfloat16)
    writes = jnp.repeat(write_rows, repeat, axis=1)
    deposit = jnp.einsum("jhp,jhn->hpn", weighted, writes, preferred_element_type=jnp.float32)
    fading = jnp.exp(cumulative[:, -1]) * (final_segment == prior_segment).astype(jnp.float32)
    return (within, inflow, fading, deposit)


def reading(read_rows, held_state, repeat):
    readers = jnp.repeat(read_rows, repeat, axis=1).astype(jnp.float32)
    return jnp.einsum("ihn,hpn->ihp", readers, held_state, precision=highest)


def gated_norm(outputs, gates, norm_scale):
    height = outputs.shape[0]
    gated = outputs * jax.nn.silu(gates.astype(jnp.float32))
    grouped = gated.reshape(height, -1, INNER // GROUPS)
    mean_square = jnp.mean(grouped * grouped, axis=-1, keepdims=True)
    normed = (grouped * lax.rsqrt(mean_square + 1e-05)).reshape(height, -1) * norm_scale
    return normed.astype(jnp.bfloat16)


def chain_states(through, local_state):

    def combine_pair(earlier, later):
        return (earlier[0] * later[0], later[0][:, None, None] * earlier[1] + later[1])

    neutral = (jnp.ones_like(through), jnp.zeros_like(local_state))
    return entering((through, local_state), "seq", combine_pair, neutral)[1]


def on_device(
    inner_input,
    state_input,
    gate_input,
    step_input,
    decay_exponent,
    skip_gain,
    documents,
    filter_inner,
    filter_state,
    norm_gain,
    output_weight,
):
    margin = KERNEL - 1
    length = documents.shape[0]
    head_count = decay_exponent.shape[0]
    groups = state_input.shape[2] // STATE
    repeat = head_count // groups
    before_inner, before_state, before_segments = passed_along(
        (inner_input[-margin:], state_input[-margin:], documents[-margin:].astype(jnp.bfloat16)),
        "seq",
        1,
    )
    segments_wide = jnp.concatenate([before_segments.astype(jnp.int32), documents])
    inner_conv = causal_conv(
        jnp.concatenate([before_inner, inner_input]), filter_inner, segments_wide, documents
    )
    state_conv = causal_conv(
        jnp.concatenate([before_state, state_input]), filter_state, segments_wide, documents
    )
    values = inner_conv.reshape(length, head_count, HEAD_DIM)
    write_rows = state_conv[:, 0].reshape(length, groups, STATE)
    read_rows = state_conv[:, 1].reshape(length, groups, STATE)
    step_size = jax.nn.softplus(step_input)
    decay_rate = -step_size * jnp.exp(decay_exponent)[:, None]
    skipped = skip_gain[None, :, None] * values.astype(jnp.float32)
    prior_segment = segments_wide[margin - 1]
    pieces = [
        span_parts(values, write_rows, read_rows, step_size, decay_rate, documents, prior_segment)
    ]
    local_state = jnp.zeros((head_count, HEAD_DIM, STATE), jnp.float32)
    through = jnp.ones((head_count,), jnp.float32)
    block_index = 0
    within, inflow, fading, deposit = pieces[block_index]
    local_state = fading[:, None, None] * local_state + deposit
    through = through * fading
    carried = chain_states(through, local_state)
    block_index = 0
    within, inflow, fading, deposit = pieces[block_index]
    outputs = within + inflow.T[:, :, None] * reading(read_rows, carried, repeat) + skipped
    scan_out = outputs.reshape(length, head_count * HEAD_DIM)
    normed = gated_norm(scan_out, gate_input, norm_gain)
    partial_value = jnp.dot(
        normed,
        lax.all_gather(output_weight, "seq", axis=1, tiled=True),
        preferred_element_type=jnp.float32,
    )
    return lax.psum_scatter(partial_value, "head", scatter_dimension=1, tiled=True).astype(
        jnp.bfloat16
    )


MESH = pl.DeviceIdType.MESH
SPAN = 256
CHANNELS = 2048
HALF = 1024
HEADS_HERE = 32
MIB = 1 << 20


def scan_kernel(
    inner_ref,
    halo_ref,
    state_ref,
    step_ref,
    decay_ref,
    skip_ref,
    marks_ref,
    rows_ref,
    filter_inner_ref,
    filter_state_ref,
    part_ref,
    infl_ref,
    dep_ref,
    read_ref,
    ext,
    conv,
    sconv,
    weighted,
):
    def convolve(source, at, halo_at, taps, target):
        lanes = pl.ds(at, 256)
        ext[0:8, :] = halo_ref[:, pl.ds(halo_at, 256)]
        ext[8:264, :] = source[:, lanes].astype(jnp.float32)
        running = marks_ref[:, 2:3] * (ext[5:261, :] * taps[0:1, lanes])
        running = running + marks_ref[:, 1:2] * (ext[6:262, :] * taps[1:2, lanes])
        running = running + marks_ref[:, 0:1] * (ext[7:263, :] * taps[2:3, lanes])
        running = running + ext[8:264, :] * taps[3:4, lanes]
        target[:, lanes] = (running * jax.nn.sigmoid(running)).astype(jnp.bfloat16)

    @pl.loop(0, CHANNELS // 256)
    def _(i):
        at = pl.multiple_of(i * 256, 256)
        convolve(inner_ref, at, at, filter_inner_ref, conv)

    @pl.loop(0, 2)
    def _(i):
        at = pl.multiple_of(i * 256, 256)
        convolve(state_ref, at, pl.multiple_of(at + CHANNELS, 256), filter_state_ref, sconv)

    read_ref[...] = sconv[:, 256:512]
    value = step_ref[...]
    step = jnp.maximum(value, 0.0) + jnp.log1p(jnp.exp(-jnp.abs(value)))
    decay = -step * jnp.exp(decay_ref[...])
    row_at = lax.broadcasted_iota(jnp.int32, (SPAN, SPAN), 0)
    col_at = lax.broadcasted_iota(jnp.int32, (SPAN, SPAN), 1)
    upper = (row_at <= col_at).astype(jnp.float32)
    cumulative = jnp.dot(
        decay, upper, precision=highest, preferred_element_type=jnp.float32
    )
    documents = rows_ref[0:1, :]
    inflow = jnp.exp(cumulative) * rows_ref[1:2, :]
    closing = jnp.exp(cumulative[:, SPAN - 1 :] - cumulative) * rows_ref[2:3, :] * step
    cum_cols = cumulative.T
    in_cols = inflow.T
    close_cols = closing.T
    linked = (marks_ref[:, 3:4] == documents) & (row_at >= col_at)
    low = lax.broadcasted_iota(jnp.int32, (SPAN, 128), 1) < HEAD_DIM
    for group in range(2):
        lanes = slice(group * 128, group * 128 + 128)
        writes = sconv[:, lanes]
        scores = lax.dot_general(
            sconv[:, 256 + group * 128 : 384 + group * 128],
            writes,
            (((1,), (1,)), ((), ())),
            preferred_element_type=jnp.float32,
        )
        scores = jnp.where(linked, scores, 0.0)
        for pair in range(8):
            first = group * 16 + pair * 2
            at = slice(first * HEAD_DIM, first * HEAD_DIM + 128)
            x = conv[:, at]

            def mixed(h):
                spread = jnp.minimum(cum_cols[:, h : h + 1] - cumulative[h : h + 1, :], 0.0)
                mixing = (jnp.exp(spread) * scores * step[h : h + 1, :]).astype(jnp.bfloat16)
                return jnp.dot(mixing, x, preferred_element_type=jnp.float32)

            def both(cols):
                return jnp.where(low, cols[:, first : first + 1], cols[:, first + 1 : first + 2])

            x32 = x.astype(jnp.float32)
            gain = jnp.where(low, skip_ref[first], skip_ref[first + 1])
            part_ref[:, at] = jnp.where(low, mixed(first), mixed(first + 1)) + gain * x32
            weighted[:, at] = (x32 * both(close_cols)).astype(jnp.bfloat16)
            infl_ref[:, at] = both(in_cols)
        wide = slice(group * HALF, group * HALF + HALF)
        dep_ref[:, wide] = lax.dot_general(
            writes,
            weighted[:, wide],
            (((0,), (0,)), ((), ())),
            preferred_element_type=jnp.float32,
        )


def mix_kernel(
    part_ref,
    infl_ref,
    dep_ref,
    read_ref,
    gate_ref,
    gain_ref,
    weight_ref,
    out_ref,
    weight_in,
    dep_stage,
    dep_in,
    fade_stage,
    fade_in,
    chain_out,
    chain_in,
    state_out,
    state_in,
    state_own,
    acts,
    partial,
    partial_own,
    sums_in,
    final_out,
    final_in,
    weight_sems,
    pair_sems,
    chain_sems,
    state_sems,
    act_send,
    act_recv,
    sum_send,
    sum_recv,
    final_send,
    final_recv,
):
    s = lax.axis_index("seq")
    h = lax.axis_index("head")
    z, y = s // 2, s % 2
    me = s * 4 + h
    z_near = z + 1 - 2 * (z % 2)
    z_far = (z + 2) % 4

    def remote(src, dst, send, recv, seq, head=h):
        return pltpu.make_async_remote_copy(
            src_ref=src,
            dst_ref=dst,
            send_sem=send,
            recv_sem=recv,
            device_id=(seq, head),
            device_id_type=MESH,
        )

    barrier = pltpu.get_barrier_semaphore()

    @pl.loop(1, 32)
    def _(i):
        other = lax.rem(me + i, 32)
        pl.semaphore_signal(
            barrier, inc=1, device_id=(other // 4, other % 4), device_id_type=MESH
        )

    pl.semaphore_wait(barrier, 31)

    y_pair = 2 * z + 1 - y
    own = pl.ds(pl.multiple_of(y * HALF, HALF), HALF)
    apart = pl.ds(pl.multiple_of((1 - y) * HALF, HALF), HALF)

    dep_stage[...] = dep_ref[:, apart].astype(jnp.bfloat16)
    fade_stage[...] = infl_ref[SPAN - 8 : SPAN, apart]
    send_dep = remote(dep_stage, dep_in, pair_sems.at[0], pair_sems.at[1], y_pair)
    send_fade = remote(fade_stage, fade_in, pair_sems.at[2], pair_sems.at[3], y_pair)
    send_fade.start()
    send_dep.start()
    send_weight = remote(
        weight_ref, weight_in, weight_sems.at[0], weight_sems.at[1], 2 * z_near + y
    )
    send_weight.start()

    @pl.when(z == 0)
    def _():
        chain_in[...] = jnp.zeros_like(chain_in)

    send_fade.wait_recv()
    send_dep.wait_recv()
    is_first = y == 0
    chain_copies = [
        remote(
            chain_out.at[q],
            chain_in.at[q],
            chain_sems.at[0, q],
            chain_sems.at[1, q],
            jnp.minimum(s + 2, 7),
        )
        for q in range(4)
    ]
    state_copies = [
        remote(state_out.at[q], state_in.at[q], state_sems.at[0, q], state_sems.at[1, q], y_pair)
        for q in range(4)
    ]
    for q in range(4):
        lanes = pl.ds(pl.multiple_of(y * HALF + q * 256, 256), 256)
        here = slice(q * 256, q * 256 + 256)
        dep_own = dep_ref[:, lanes]
        dep_other = dep_in[:, here].astype(jnp.float32)
        fade_own = infl_ref[SPAN - 1 : SPAN, lanes]
        fade_other = fade_in[7:8, here]
        dep_0 = jnp.where(is_first, dep_own, dep_other)
        dep_1 = jnp.where(is_first, dep_other, dep_own)
        fade_0 = jnp.where(is_first, fade_own, fade_other)
        fade_1 = jnp.where(is_first, fade_other, fade_own)
        slab = fade_1 * dep_0 + dep_1
        slab_fade = fade_0 * fade_1

        @pl.when(z > 0)
        def _():
            chain_copies[q].wait_recv()

        entering_0 = chain_in[q].astype(jnp.float32)
        chain_out[q] = (slab_fade * entering_0 + slab).astype(jnp.bfloat16)

        @pl.when(z < 3)
        def _():
            chain_copies[q].start()

        entering_1 = fade_0 * entering_0 + dep_0
        state_own[:, here] = jnp.where(is_first, entering_0, entering_1).astype(jnp.bfloat16)
        state_out[q] = jnp.where(is_first, entering_1, entering_0).astype(jnp.bfloat16)
        state_copies[q].start()

    def norm_half(half, state):
        lanes = pl.ds(pl.multiple_of(half * HALF, HALF), HALF)
        reads_at = pl.ds(pl.multiple_of(half * 128, 128), 128)

        @pl.loop(0, 4)
        def _(i):
            rows = pl.ds(pl.multiple_of(i * 64, 64), 64)
            read = jnp.dot(read_ref[rows, reads_at], state, preferred_element_type=jnp.float32)
            gate = gate_ref[rows, lanes].astype(jnp.float32)
            scan = part_ref[rows, lanes] + infl_ref[rows, lanes] * read
            gated = scan * (gate * jax.nn.sigmoid(gate))
            mean = jnp.sum(gated * gated, axis=1, keepdims=True) * (1.0 / HALF)
            normed = gated * lax.rsqrt(mean + 1e-05) * gain_ref[:, lanes]
            acts[0, half, rows, :] = normed.astype(jnp.bfloat16)

    def send_act(slot, half, source, seq):
        return remote(
            acts.at[source, half],
            acts.at[slot, half],
            act_send.at[slot - 1, half],
            act_recv.at[slot - 1, half],
            seq,
        )

    z_pair = 2 * z_far + y
    norm_half(y, state_own[...])
    send_act(2, y, 0, z_pair).start()
    send_act(1, y, 0, y_pair).start()
    for q in range(4):
        state_copies[q].wait_recv()
    norm_half(1 - y, jnp.concatenate([state_in[q] for q in range(4)], axis=1))
    send_act(2, 1 - y, 0, z_pair).start()
    send_act(1, 1 - y, 0, y_pair).start()

    def sum_copy(k, o):
        to = h ^ o
        rows = pl.ds(pl.multiple_of(to * 64, 64), 64)
        return remote(
            partial.at[k, rows],
            sums_in.at[k, o - 1],
            sum_send.at[k, o - 1],
            sum_recv.at[k, o - 1],
            s,
            to,
        )

    def project(k):
        for side, weight in enumerate((weight_ref, weight_in)):

            @pl.loop(0, 2)
            def _(i):
                lanes = pl.ds(pl.multiple_of(i * 256, 256), 256)
                spot = pl.ds(pl.multiple_of(side * 512 + i * 256, 256), 256)
                total = jnp.dot(
                    acts[k, 0], weight[0:HALF, lanes], preferred_element_type=jnp.float32
                ) + jnp.dot(
                    acts[k, 1], weight[HALF:CHANNELS, lanes], preferred_element_type=jnp.float32
                )
                partial_own[k, :, spot] = total
                partial[k, :, spot] = total.astype(jnp.bfloat16)

        for o in (2, 3, 1):
            sum_copy(k, o).start()

    def final_parts(k):
        zt = z if k < 2 else z_far
        yt = y if k % 2 == 0 else 1 - y
        rows = pl.ds(pl.multiple_of(h * 64, 64), 64)
        spot = pl.ds(pl.multiple_of(y * 512, 512), 512)
        parts = []
        for side, head in enumerate((z, z_near)):
            target = 2 * zt + yt
            stays = (target == s) & (head == h)
            copy = remote(
                final_out.at[k, side],
                final_in.at[rows, spot],
                final_send.at[k, side],
                final_recv.at[y * 4 + h],
                target,
                head,
            )
            parts.append((side, stays, copy))
        return rows, spot, parts

    def finish(k):
        for o in (1, 2, 3):
            sum_copy(k, o).wait_recv()
        rows, spot, parts = final_parts(k)
        total = partial_own[k, rows, :]
        for o in range(3):
            total = total + sums_in[k, o].astype(jnp.float32)
        total = total.astype(jnp.bfloat16)
        for side, stays, copy in parts:
            final_out[k, side] = total[:, side * 512 : side * 512 + 512]

            @pl.when(stays)
            def _():
                final_in[rows, spot] = total[:, side * 512 : side * 512 + 512]

            @pl.when(jnp.logical_not(stays))
            def _():
                copy.start()

    send_weight.wait_recv()
    project(0)
    send_act(1, 1 - y, 0, y_pair).wait_recv()
    send_act(1, y, 0, y_pair).wait_recv()
    project(1)
    for half in (y, 1 - y):
        send_act(2, half, 0, z_pair).wait_recv()
        send_act(3, half, 2, y_pair).start()
    finish(0)
    project(2)
    finish(1)
    send_act(3, 1 - y, 2, y_pair).wait_recv()
    send_act(3, y, 2, y_pair).wait_recv()
    project(3)
    finish(2)
    finish(3)

    z_from = 2 * (h // 2) + z % 2
    for y_from in range(2):
        for h_from in range(4):
            rows = slice(h_from * 64, h_from * 64 + 64)
            spot = slice(y_from * 512, y_from * 512 + 512)
            mine = (z_from == z) & (y_from == y) & (h_from == h)

            @pl.when(jnp.logical_not(mine))
            def _():
                remote(
                    final_out.at[0, 0],
                    final_in.at[rows, spot],
                    final_send.at[0, 0],
                    final_recv.at[y_from * 4 + h_from],
                    2 * z_from + y_from,
                    h_from,
                ).wait_recv()

    out_ref[...] = final_in[...]

    send_dep.wait_send()
    send_fade.wait_send()
    send_weight.wait_send()
    for q in range(4):
        state_copies[q].wait_send()

        @pl.when(z < 3)
        def _():
            chain_copies[q].wait_send()

    for half in range(2):
        send_act(1, half, 0, y_pair).wait_send()
        send_act(2, half, 0, z_pair).wait_send()
        send_act(3, half, 2, y_pair).wait_send()
    for k in range(4):
        for o in (1, 2, 3):
            sum_copy(k, o).wait_send()
        for side, stays, copy in final_parts(k)[2]:

            @pl.when(jnp.logical_not(stays))
            def _():
                copy.wait_send()


def on_device_fast(
    inner_input,
    state_input,
    gate_input,
    step_input,
    decay_exponent,
    skip_gain,
    documents,
    filter_inner,
    filter_state,
    norm_gain,
    output_weight,
):
    margin = KERNEL - 1
    state_flat = state_input.reshape(SPAN, 512)
    edge = jnp.concatenate(
        [
            inner_input[-margin:],
            state_flat[-margin:],
            jnp.broadcast_to(documents[-margin:, None].astype(jnp.bfloat16), (margin, 128)),
        ],
        axis=1,
    )
    before = passed_along(edge, "seq", 1).astype(jnp.float32)
    halo = jnp.pad(before, ((8 - margin, 0), (0, 0)))
    docs = documents.astype(jnp.float32)
    wide = jnp.concatenate([before[:, CHANNELS + 512], docs])
    marks = [(wide[margin - k : margin - k + SPAN] == docs).astype(jnp.float32) for k in (1, 2, 3)]
    marks = jnp.stack(marks + [docs] * 5, axis=1)
    rows = jnp.stack(
        [docs, (docs == wide[margin - 1]).astype(jnp.float32)]
        + [(docs == docs[-1]).astype(jnp.float32)] * 6
    )
    vmem = pl.BlockSpec(memory_space=pltpu.VMEM)
    smem = pl.BlockSpec(memory_space=pltpu.SMEM)
    part, infl, dep, reads = pl.pallas_call(
        scan_kernel,
        out_shape=(
            jax.ShapeDtypeStruct((SPAN, CHANNELS), jnp.float32),
            jax.ShapeDtypeStruct((SPAN, CHANNELS), jnp.float32),
            jax.ShapeDtypeStruct((STATE, CHANNELS), jnp.float32),
            jax.ShapeDtypeStruct((SPAN, 256), jnp.bfloat16),
        ),
        in_specs=[vmem] * 5 + [smem] + [vmem] * 4,
        out_specs=(vmem,) * 4,
        scratch_shapes=[
            pltpu.VMEM((SPAN + 8, 256), jnp.float32),
            pltpu.VMEM((SPAN, CHANNELS), jnp.bfloat16),
            pltpu.VMEM((SPAN, 512), jnp.bfloat16),
            pltpu.VMEM((SPAN, CHANNELS), jnp.bfloat16),
        ],
        compiler_params=pltpu.CompilerParams(vmem_limit_bytes=48 * MIB),
        name="scan_local",
    )(
        inner_input,
        halo,
        state_flat,
        step_input,
        decay_exponent[:, None],
        skip_gain,
        marks,
        rows,
        filter_inner,
        filter_state.reshape(KERNEL, 512),
    )
    bf16, f32 = jnp.bfloat16, jnp.float32
    dma = pltpu.SemaphoreType.DMA
    return pl.pallas_call(
        mix_kernel,
        out_shape=jax.ShapeDtypeStruct((SPAN, 1024), bf16),
        in_specs=[vmem] * 7,
        out_specs=vmem,
        scratch_shapes=[
            pltpu.VMEM((CHANNELS, 512), bf16),
            pltpu.VMEM((STATE, HALF), bf16),
            pltpu.VMEM((STATE, HALF), bf16),
            pltpu.VMEM((8, HALF), f32),
            pltpu.VMEM((8, HALF), f32),
            pltpu.VMEM((4, STATE, 256), bf16),
            pltpu.VMEM((4, STATE, 256), bf16),
            pltpu.VMEM((4, STATE, 256), bf16),
            pltpu.VMEM((4, STATE, 256), bf16),
            pltpu.VMEM((STATE, HALF), bf16),
            pltpu.VMEM((4, 2, SPAN, HALF), bf16),
            pltpu.VMEM((4, SPAN, 1024), bf16),
            pltpu.VMEM((4, SPAN, 1024), f32),
            pltpu.VMEM((4, 3, 64, 1024), bf16),
            pltpu.VMEM((4, 2, 64, 512), bf16),
            pltpu.VMEM((SPAN, 1024), bf16),
            dma((2,)),
            dma((4,)),
            dma((2, 4)),
            dma((2, 4)),
            dma((3, 2)),
            dma((3, 2)),
            dma((4, 3)),
            dma((4, 3)),
            dma((4, 2)),
            dma((8,)),
        ],
        compiler_params=pltpu.CompilerParams(
            vmem_limit_bytes=56 * MIB, collective_id=0, has_side_effects=True
        ),
        name="mix_exchange",
    )(part, infl, dep, reads, gate_input, norm_gain[None, :], output_weight)


def solution(mesh):
    placed = (
        P("seq", "head"),
        P("seq", None, "head"),
        P("seq", "head"),
        P("head", "seq"),
        P("head"),
        P("head"),
        P("seq"),
        P(None, "head"),
        P(None, None, "head"),
        P("head"),
        P("head", "seq"),
    )
    ways = dict(mesh.shape)
    fast = ways["seq"] == 8 and ways["head"] == 4
    return jax.shard_map(
        on_device_fast if fast else on_device, mesh=mesh, in_specs=placed, out_specs=P("seq", "head"), check_vma=False
    )
```

```python
import jax
import jax.numpy as jnp
from jax import lax
from jax.experimental import pallas as pl
from jax.experimental.pallas import tpu as pltpu
from jax.sharding import PartitionSpec as P

HEAD_DIM = 64
STATE = 128
GROUPS = 8
INNER = 8192
KERNEL = 4


highest = lax.Precision.HIGHEST


def entering(part, axis, combine, identity):
    place = lax.axis_index(axis)
    gathered = jax.tree.map(lambda a: lax.all_gather(a, axis), part)
    state = jax.tree.map(lambda a, e: jnp.zeros_like(a) + jnp.asarray(e, a.dtype), part, identity)

    def one(step, state):
        return combine(
            state, jax.tree.map(lambda a: lax.dynamic_index_in_dim(a, step, 0, False), gathered)
        )

    return lax.fori_loop(0, place, one, state)


def passed_along(value, axis, steps):
    count = lax.axis_size(axis)
    initial, last = (max(0, -steps), min(count, count - steps))
    return lax.ppermute(value, axis, [(source, source + steps) for source in range(initial, last)])


def causal_conv(extended, weights, segments_wide, segment_block):
    length = segment_block.shape[0]
    running = jnp.zeros(extended[:length].shape, jnp.float32)
    for offset in range(KERNEL):
        window = extended[offset : offset + length].astype(jnp.float32)
        matches = segments_wide[offset : offset + length] == segment_block
        matches = matches.reshape((length,) + (1,) * (extended.ndim - 1))
        running = running + jnp.where(matches, window * weights[offset], jnp.float32(0.0))
    return jax.nn.silu(running).astype(jnp.bfloat16)


def span_parts(values, write_rows, read_rows, step_size, decay_rate, segment_block, prior_segment):
    length = segment_block.shape[0]
    repeat = decay_rate.shape[0] // write_rows.shape[1]
    cumulative = jnp.cumsum(decay_rate, axis=1)
    places = jnp.arange(length)
    linked = (segment_block[:, None] == segment_block[None, :]) & (
        places[:, None] >= places[None, :]
    )
    spread = cumulative[:, :, None] - cumulative[:, None, :]
    decays = jnp.exp(jnp.where(linked[None], spread, -jnp.inf))
    scores = jnp.einsum("ign,jgn->gij", read_rows, write_rows, preferred_element_type=jnp.float32)
    scores = jnp.repeat(scores, repeat, axis=0)
    mixing = (decays * scores * step_size[:, None, :]).astype(jnp.bfloat16)
    within = jnp.einsum("hij,jhp->ihp", mixing, values, preferred_element_type=jnp.float32)
    inflow = jnp.exp(cumulative) * (segment_block == prior_segment)[None, :].astype(jnp.float32)
    final_segment = segment_block[-1]
    closing = (
        jnp.exp(cumulative[:, -1:] - cumulative)
        * (segment_block == final_segment)[None, :].astype(jnp.float32)
        * step_size
    )
    weighted = (values.astype(jnp.float32) * closing.T[:, :, None]).astype(jnp.bfloat16)
    writes = jnp.repeat(write_rows, repeat, axis=1)
    deposit = jnp.einsum("jhp,jhn->hpn", weighted, writes, preferred_element_type=jnp.float32)
    fading = jnp.exp(cumulative[:, -1]) * (final_segment == prior_segment).astype(jnp.float32)
    return (within, inflow, fading, deposit)


def reading(read_rows, held_state, repeat):
    readers = jnp.repeat(read_rows, repeat, axis=1).astype(jnp.float32)
    return jnp.einsum("ihn,hpn->ihp", readers, held_state, precision=highest)


def gated_norm(outputs, gates, norm_scale):
    height = outputs.shape[0]
    gated = outputs * jax.nn.silu(gates.astype(jnp.float32))
    grouped = gated.reshape(height, -1, INNER // GROUPS)
    mean_square = jnp.mean(grouped * grouped, axis=-1, keepdims=True)
    normed = (grouped * lax.rsqrt(mean_square + 1e-05)).reshape(height, -1) * norm_scale
    return normed.astype(jnp.bfloat16)


def chain_states(through, local_state):

    def combine_pair(earlier, later):
        return (earlier[0] * later[0], later[0][:, None, None] * earlier[1] + later[1])

    neutral = (jnp.ones_like(through), jnp.zeros_like(local_state))
    return entering((through, local_state), "seq", combine_pair, neutral)[1]


def on_device(
    inner_input,
    state_input,
    gate_input,
    step_input,
    decay_exponent,
    skip_gain,
    documents,
    filter_inner,
    filter_state,
    norm_gain,
    output_weight,
):
    margin = KERNEL - 1
    length = documents.shape[0]
    head_count = decay_exponent.shape[0]
    groups = state_input.shape[2] // STATE
    repeat = head_count // groups
    before_inner, before_state, before_segments = passed_along(
        (inner_input[-margin:], state_input[-margin:], documents[-margin:].astype(jnp.bfloat16)),
        "seq",
        1,
    )
    segments_wide = jnp.concatenate([before_segments.astype(jnp.int32), documents])
    inner_conv = causal_conv(
        jnp.concatenate([before_inner, inner_input]), filter_inner, segments_wide, documents
    )
    state_conv = causal_conv(
        jnp.concatenate([before_state, state_input]), filter_state, segments_wide, documents
    )
    values = inner_conv.reshape(length, head_count, HEAD_DIM)
    write_rows = state_conv[:, 0].reshape(length, groups, STATE)
    read_rows = state_conv[:, 1].reshape(length, groups, STATE)
    step_size = jax.nn.softplus(step_input)
    decay_rate = -step_size * jnp.exp(decay_exponent)[:, None]
    skipped = skip_gain[None, :, None] * values.astype(jnp.float32)
    prior_segment = segments_wide[margin - 1]
    pieces = [
        span_parts(values, write_rows, read_rows, step_size, decay_rate, documents, prior_segment)
    ]
    local_state = jnp.zeros((head_count, HEAD_DIM, STATE), jnp.float32)
    through = jnp.ones((head_count,), jnp.float32)
    block_index = 0
    within, inflow, fading, deposit = pieces[block_index]
    local_state = fading[:, None, None] * local_state + deposit
    through = through * fading
    carried = chain_states(through, local_state)
    block_index = 0
    within, inflow, fading, deposit = pieces[block_index]
    outputs = within + inflow.T[:, :, None] * reading(read_rows, carried, repeat) + skipped
    scan_out = outputs.reshape(length, head_count * HEAD_DIM)
    normed = gated_norm(scan_out, gate_input, norm_gain)
    partial_value = jnp.dot(
        normed,
        lax.all_gather(output_weight, "seq", axis=1, tiled=True),
        preferred_element_type=jnp.float32,
    )
    return lax.psum_scatter(partial_value, "head", scatter_dimension=1, tiled=True).astype(
        jnp.bfloat16
    )


MESH = pl.DeviceIdType.MESH
SPAN = 256
CHANNELS = 2048
HALF = 1024
MIB = 1 << 20


def fused_kernel(
    inner_ref,
    state_ref,
    step_ref,
    decay_ref,
    documents_ref,
    filter_inner_ref,
    filter_state_ref,
    gain_ref,
    skip_ref,
    gate_hbm,
    weight_hbm,
    out_ref,
    gate_ref,
    weight_ref,
    weight_in,
    halo_inner,
    halo_state,
    halo_documents,
    ext,
    conv,
    sconv,
    cum_rows,
    step_rows,
    in_rows,
    close_rows,
    weighted,
    part_ref,
    infl_ref,
    dep_ref,
    dep_stage,
    dep_in,
    fade_stage,
    fade_in,
    chain_out,
    chain_in,
    state_out,
    state_in,
    state_own,
    acts,
    partial,
    partial_own,
    sums_in,
    final_out,
    final_in,
    local_sems,
    halo_sems,
    weight_sems,
    pair_sems,
    chain_sems,
    state_sems,
    act_send,
    act_recv,
    sum_send,
    sum_recv,
    final_send,
    final_recv,
):
    s = lax.axis_index("seq")
    h = lax.axis_index("head")
    z, y = s // 2, s % 2
    me = s * 4 + h
    z_near = z + 1 - 2 * (z % 2)
    z_far = (z + 2) % 4
    y_pair = 2 * z + 1 - y
    z_pair = 2 * z_far + y

    def remote(src, dst, send, recv, seq, head=h):
        return pltpu.make_async_remote_copy(
            src_ref=src,
            dst_ref=dst,
            send_sem=send,
            recv_sem=recv,
            device_id=(seq, head),
            device_id_type=MESH,
        )

    gate_copy = pltpu.make_async_copy(gate_hbm, gate_ref, local_sems.at[0])
    weight_copy = pltpu.make_async_copy(weight_hbm, weight_ref, local_sems.at[1])
    gate_copy.start()
    weight_copy.start()

    barrier = pltpu.get_barrier_semaphore()

    @pl.loop(1, 32)
    def _(i):
        other = lax.rem(me + i, 32)
        pl.semaphore_signal(
            barrier, inc=1, device_id=(other // 4, other % 4), device_id_type=MESH
        )

    pl.semaphore_wait(barrier, 31)

    after = jnp.minimum(s + 1, 7)
    halo_copies = [
        remote(source, target, halo_sems.at[0, i], halo_sems.at[1, i], after)
        for i, (source, target) in enumerate(
            (
                (documents_ref, halo_documents),
                (state_ref.at[pl.ds(SPAN - 16, 16)], halo_state),
                (inner_ref.at[pl.ds(SPAN - 16, 16)], halo_inner),
            )
        )
    ]

    @pl.when(s < 7)
    def _():
        for copy in halo_copies:
            copy.start()

    weight_copies = []
    for i in range(4):
        rows = pl.ds(i * 512, 512)
        weight_copies.append(
            remote(
                weight_hbm.at[rows],
                weight_in.at[rows],
                weight_sems.at[0, i],
                weight_sems.at[1, i],
                2 * z_near + y,
            )
        )
    weight_copies[0].start()

    @pl.when(z % 2 == 1)
    def _():
        for copy in weight_copies[1:]:
            copy.start()

    @pl.when(s == 0)
    def _():
        halo_documents[...] = jnp.zeros_like(halo_documents)
        halo_state[...] = jnp.zeros_like(halo_state)
        halo_inner[...] = jnp.zeros_like(halo_inner)

    diagonal = lax.broadcasted_iota(jnp.int32, (32, 32), 0) == lax.broadcasted_iota(
        jnp.int32, (32, 32), 1
    )
    rate = jnp.sum(
        jnp.where(diagonal, jnp.broadcast_to(jnp.exp(decay_ref[...]), (32, 32)), 0.0),
        axis=1,
        keepdims=True,
    )
    value = step_ref[...]
    step = jnp.maximum(value, 0.0) + jnp.log1p(jnp.exp(-jnp.abs(value)))
    row_at = lax.broadcasted_iota(jnp.int32, (SPAN, SPAN), 0)
    col_at = lax.broadcasted_iota(jnp.int32, (SPAN, SPAN), 1)
    upper = (row_at <= col_at).astype(jnp.float32)
    cumulative = jnp.dot(
        -step * rate, upper, precision=highest, preferred_element_type=jnp.float32
    )
    documents = documents_ref[...].astype(jnp.float32)
    final = (documents == documents[:, SPAN - 1 :]).astype(jnp.float32)
    step_rows[...] = step
    cum_rows[...] = cumulative
    close_rows[...] = jnp.exp(cumulative[:, SPAN - 1 :] - cumulative) * final * step

    @pl.when(s > 0)
    def _():
        for copy in halo_copies:
            copy.wait_recv()

    before = halo_documents[...].astype(jnp.float32)
    in_rows[...] = jnp.exp(cumulative) * (documents == before[:, SPAN - 1 :]).astype(jnp.float32)
    lane = lax.broadcasted_iota(jnp.int32, (8, SPAN), 1)
    mark_row = lax.broadcasted_iota(jnp.int32, (8, SPAN), 0)
    documents_8 = jnp.broadcast_to(documents, (8, SPAN))
    before_8 = jnp.broadcast_to(before, (8, SPAN))
    mark_rows = documents_8
    for k in (1, 2, 3):
        shifted = jnp.where(
            lane < k, pltpu.roll(before_8, k, axis=1), pltpu.roll(documents_8, k, axis=1)
        )
        same = (shifted == documents_8).astype(jnp.float32)
        mark_rows = jnp.where(mark_row == k, same, mark_rows)
    marks = mark_rows.T

    def convolve(source, halo, at, taps, target):
        lanes = pl.ds(at, 256)
        ext[0:16, :] = halo[:, lanes].astype(jnp.float32)
        ext[16:272, :] = source[:, lanes].astype(jnp.float32)
        running = marks[:, 3:4] * (ext[13:269, :] * taps[0:1, lanes])
        running = running + marks[:, 2:3] * (ext[14:270, :] * taps[1:2, lanes])
        running = running + marks[:, 1:2] * (ext[15:271, :] * taps[2:3, lanes])
        running = running + ext[16:272, :] * taps[3:4, lanes]
        target[:, lanes] = (running * jax.nn.sigmoid(running)).astype(jnp.bfloat16)

    @pl.loop(0, 2)
    def _(i):
        convolve(state_ref, halo_state, pl.multiple_of(i * 256, 256), filter_state_ref, sconv)

    linked = (marks[:, 0:1] == documents) & (row_at >= col_at)
    low = lax.broadcasted_iota(jnp.int32, (SPAN, 128), 1) < HEAD_DIM

    apart = pl.ds(pl.multiple_of((1 - y) * HALF, HALF), HALF)
    send_dep = remote(dep_stage, dep_in, pair_sems.at[0], pair_sems.at[1], y_pair)
    send_fade = remote(fade_stage, fade_in, pair_sems.at[2], pair_sems.at[3], y_pair)

    @pl.loop(0, 2)
    def _(turn):
        group = jnp.where(turn == 0, 1 - y, y)
        base = group * HALF

        @pl.loop(0, 4)
        def _(i):
            at = pl.multiple_of(base + i * 256, 256)
            convolve(inner_ref, halo_inner, at, filter_inner_ref, conv)

        writes = sconv[:, pl.ds(pl.multiple_of(group * 128, 128), 128)]
        reads = sconv[:, pl.ds(pl.multiple_of(256 + group * 128, 128), 128)]
        scores = lax.dot_general(
            reads, writes, (((1,), (1,)), ((), ())), preferred_element_type=jnp.float32
        )
        scores = jnp.where(linked, scores, 0.0)
        heads = pl.ds(pl.multiple_of(group * 16, 16), 16)
        cums = cum_rows[heads, :]
        steps = step_rows[heads, :]
        cum_cols = cums.T
        in_cols = in_rows[heads, :].T
        close_cols = close_rows[heads, :].T
        for pair in range(8):
            first = pair * 2
            at = pl.ds(pl.multiple_of(base + pair * 128, 128), 128)
            x = conv[:, at]

            def mixed(j):
                spread = jnp.minimum(cum_cols[:, j : j + 1] - cums[j : j + 1, :], 0.0)
                mixing = (jnp.exp(spread) * scores * steps[j : j + 1, :]).astype(jnp.bfloat16)
                return jnp.dot(mixing, x, preferred_element_type=jnp.float32)

            def both(cols):
                return jnp.where(low, cols[:, first : first + 1], cols[:, first + 1 : first + 2])

            x32 = x.astype(jnp.float32)
            gain = jnp.where(low, skip_ref[group * 16 + first], skip_ref[group * 16 + first + 1])
            part_ref[:, at] = jnp.where(low, mixed(first), mixed(first + 1)) + gain * x32
            weighted[:, pair * 128 : pair * 128 + 128] = (x32 * both(close_cols)).astype(
                jnp.bfloat16
            )
            infl_ref[:, at] = both(in_cols)
        dep_ref[...] = lax.dot_general(
            writes, weighted[...], (((0,), (0,)), ((), ())), preferred_element_type=jnp.float32
        )

        @pl.when(turn == 0)
        def _():
            dep_stage[...] = dep_ref[...].astype(jnp.bfloat16)
            fade_stage[...] = infl_ref[SPAN - 8 : SPAN, apart]
            send_fade.start()
            send_dep.start()

    @pl.when(z == 0)
    def _():
        chain_in[...] = jnp.zeros_like(chain_in)

    send_fade.wait_recv()
    send_dep.wait_recv()
    is_first = y == 0
    chain_copies = [
        remote(
            chain_out.at[q],
            chain_in.at[q],
            chain_sems.at[0, q],
            chain_sems.at[1, q],
            jnp.minimum(s + 2, 7),
        )
        for q in range(4)
    ]
    state_copies = [
        remote(state_out.at[q], state_in.at[q], state_sems.at[0, q], state_sems.at[1, q], y_pair)
        for q in range(4)
    ]
    for q in range(4):
        lanes = pl.ds(pl.multiple_of(y * HALF + q * 256, 256), 256)
        here = slice(q * 256, q * 256 + 256)
        dep_own = dep_ref[:, here]
        dep_other = dep_in[:, here].astype(jnp.float32)
        fade_own = infl_ref[SPAN - 8 : SPAN, lanes][7:8]
        fade_other = fade_in[7:8, here]
        dep_0 = jnp.where(is_first, dep_own, dep_other)
        dep_1 = jnp.where(is_first, dep_other, dep_own)
        fade_0 = jnp.where(is_first, fade_own, fade_other)
        fade_1 = jnp.where(is_first, fade_other, fade_own)
        slab = fade_1 * dep_0 + dep_1
        slab_fade = fade_0 * fade_1

        @pl.when(z > 0)
        def _():
            chain_copies[q].wait_recv()

        entering_0 = chain_in[q].astype(jnp.float32)
        chain_out[q] = (slab_fade * entering_0 + slab).astype(jnp.bfloat16)

        @pl.when(z < 3)
        def _():
            chain_copies[q].start()

        entering_1 = fade_0 * entering_0 + dep_0
        state_own[:, here] = jnp.where(is_first, entering_0, entering_1).astype(jnp.bfloat16)
        state_out[q] = jnp.where(is_first, entering_1, entering_0).astype(jnp.bfloat16)
        state_copies[q].start()

    @pl.when(z % 2 == 0)
    def _():
        for copy in weight_copies[1:]:
            copy.start()

    gate_copy.wait()

    def act_copy(slot, half, quarter):
        source = 2 if slot == 3 else 0
        rows = pl.ds(quarter * 128, 128)
        return remote(
            acts.at[source, half, rows],
            acts.at[slot, half, rows],
            act_send.at[slot - 1, half, quarter],
            act_recv.at[slot - 1, half, quarter],
            z_pair if slot == 2 else y_pair,
        )

    def norm_half(half, state):
        lanes = pl.ds(pl.multiple_of(half * HALF, HALF), HALF)
        reads_at = pl.ds(pl.multiple_of(256 + half * 128, 128), 128)
        for quarter in range(2):

            @pl.loop(0, 2)
            def _(i):
                rows = pl.ds(pl.multiple_of(quarter * 128 + i * 64, 64), 64)
                read = jnp.dot(sconv[rows, reads_at], state, preferred_element_type=jnp.float32)
                gate = gate_ref[rows, lanes].astype(jnp.float32)
                scan = part_ref[rows, lanes] + infl_ref[rows, lanes] * read
                gated = scan * (gate * jax.nn.sigmoid(gate))
                mean = jnp.sum(gated * gated, axis=1, keepdims=True) * (1.0 / HALF)
                normed = gated * lax.rsqrt(mean + 1e-05) * gain_ref[:, lanes]
                acts[0, half, rows, :] = normed.astype(jnp.bfloat16)

            act_copy(2, half, quarter).start()
            act_copy(1, half, quarter).start()

    norm_half(y, state_own[...])
    for q in range(4):
        state_copies[q].wait_recv()
    norm_half(1 - y, jnp.concatenate([state_in[q] for q in range(4)], axis=1))

    def sum_copy(k, side, o):
        to = h ^ o
        rows = pl.ds(pl.multiple_of(to * 64, 64), 64)
        return remote(
            partial.at[k, side, rows],
            sums_in.at[k, side, o - 1],
            sum_send.at[k, side, o - 1],
            sum_recv.at[k, side, o - 1],
            s,
            to,
        )

    def project(k, side):
        weight = (weight_ref, weight_in)[side]

        @pl.loop(0, 2)
        def _(i):
            lanes = pl.ds(pl.multiple_of(i * 256, 256), 256)
            total = jnp.dot(
                acts[k, 0], weight[0:HALF, lanes], preferred_element_type=jnp.float32
            ) + jnp.dot(
                acts[k, 1], weight[HALF:CHANNELS, lanes], preferred_element_type=jnp.float32
            )
            partial_own[k, side, :, lanes] = total
            partial[k, side, :, lanes] = total.astype(jnp.bfloat16)

        for o in (2, 3, 1):
            sum_copy(k, side, o).start()

    def final_part(k, side):
        zt = z if k < 2 else z_far
        yt = y if k % 2 == 0 else 1 - y
        head = (z, z_near)[side]
        target = 2 * zt + yt
        stays = (target == s) & (head == h)
        rows = pl.ds(pl.multiple_of(h * 64, 64), 64)
        spot = pl.ds(pl.multiple_of(y * 512, 512), 512)
        copy = remote(
            final_out.at[k, side],
            final_in.at[rows, spot],
            final_send.at[k, side],
            final_recv.at[y * 4 + h],
            target,
            head,
        )
        return rows, spot, stays, copy

    def finish(k, side):
        for o in (1, 2, 3):
            sum_copy(k, side, o).wait_recv()
        rows, spot, stays, copy = final_part(k, side)
        total = partial_own[k, side, rows, :]
        for o in range(3):
            total = total + sums_in[k, side, o].astype(jnp.float32)
        total = total.astype(jnp.bfloat16)
        final_out[k, side] = total

        @pl.when(stays)
        def _():
            final_in[rows, spot] = total

        @pl.when(jnp.logical_not(stays))
        def _():
            copy.start()

    def arrived(slot, half):
        for quarter in range(2):
            act_copy(slot, half, quarter).wait_recv()
            if slot == 2:
                act_copy(3, half, quarter).start()

    weight_copy.wait()
    project(0, 0)
    arrived(1, 1 - y)
    arrived(1, y)
    project(1, 0)
    finish(0, 0)
    arrived(2, y)
    for copy in weight_copies:
        copy.wait_recv()
    project(0, 1)
    finish(1, 0)
    project(1, 1)
    finish(0, 1)
    arrived(2, 1 - y)
    project(2, 0)
    finish(1, 1)
    project(2, 1)
    finish(2, 0)
    arrived(3, 1 - y)
    arrived(3, y)
    project(3, 0)
    finish(2, 1)
    project(3, 1)
    finish(3, 0)
    finish(3, 1)

    z_from = 2 * (h // 2) + z % 2
    for y_from in range(2):
        for h_from in range(4):
            rows = slice(h_from * 64, h_from * 64 + 64)
            spot = slice(y_from * 512, y_from * 512 + 512)
            mine = (z_from == z) & (y_from == y) & (h_from == h)

            @pl.when(jnp.logical_not(mine))
            def _():
                remote(
                    final_out.at[0, 0],
                    final_in.at[rows, spot],
                    final_send.at[0, 0],
                    final_recv.at[y_from * 4 + h_from],
                    2 * z_from + y_from,
                    h_from,
                ).wait_recv()

    out_ref[...] = final_in[...]

    @pl.when(s < 7)
    def _():
        for copy in halo_copies:
            copy.wait_send()

    send_dep.wait_send()
    send_fade.wait_send()
    for q in range(4):
        weight_copies[q].wait_send()
        state_copies[q].wait_send()

        @pl.when(z < 3)
        def _():
            chain_copies[q].wait_send()

    for slot in (1, 2, 3):
        for half in range(2):
            for quarter in range(2):
                act_copy(slot, half, quarter).wait_send()
    for k in range(4):
        for side in range(2):
            for o in (1, 2, 3):
                sum_copy(k, side, o).wait_send()
            stays, copy = final_part(k, side)[2:]

            @pl.when(jnp.logical_not(stays))
            def _():
                copy.wait_send()


def on_device_fast(
    inner_input,
    state_input,
    gate_input,
    step_input,
    decay_exponent,
    skip_gain,
    documents,
    filter_inner,
    filter_state,
    norm_gain,
    output_weight,
):
    vmem = pl.BlockSpec(memory_space=pltpu.VMEM)
    smem = pl.BlockSpec(memory_space=pltpu.SMEM)
    anywhere = pl.BlockSpec(memory_space=pl.ANY)
    bf16, f32 = jnp.bfloat16, jnp.float32
    dma = pltpu.SemaphoreType.DMA
    return pl.pallas_call(
        fused_kernel,
        out_shape=jax.ShapeDtypeStruct((SPAN, 1024), bf16),
        in_specs=[vmem] * 8 + [smem] + [anywhere] * 2,
        out_specs=vmem,
        scratch_shapes=[
            pltpu.VMEM((SPAN, CHANNELS), bf16),
            pltpu.VMEM((CHANNELS, 512), bf16),
            pltpu.VMEM((CHANNELS, 512), bf16),
            pltpu.VMEM((16, CHANNELS), bf16),
            pltpu.VMEM((16, 512), bf16),
            pltpu.VMEM((1, SPAN), jnp.int32),
            pltpu.VMEM((SPAN + 16, 256), f32),
            pltpu.VMEM((SPAN, CHANNELS), bf16),
            pltpu.VMEM((SPAN, 512), bf16),
            pltpu.VMEM((32, SPAN), f32),
            pltpu.VMEM((32, SPAN), f32),
            pltpu.VMEM((32, SPAN), f32),
            pltpu.VMEM((32, SPAN), f32),
            pltpu.VMEM((SPAN, HALF), bf16),
            pltpu.VMEM((SPAN, CHANNELS), f32),
            pltpu.VMEM((SPAN, CHANNELS), f32),
            pltpu.VMEM((STATE, HALF), f32),
            pltpu.VMEM((STATE, HALF), bf16),
            pltpu.VMEM((STATE, HALF), bf16),
            pltpu.VMEM((8, HALF), f32),
            pltpu.VMEM((8, HALF), f32),
            pltpu.VMEM((4, STATE, 256), bf16),
            pltpu.VMEM((4, STATE, 256), bf16),
            pltpu.VMEM((4, STATE, 256), bf16),
            pltpu.VMEM((4, STATE, 256), bf16),
            pltpu.VMEM((STATE, HALF), bf16),
            pltpu.VMEM((4, 2, SPAN, HALF), bf16),
            pltpu.VMEM((4, 2, SPAN, 512), bf16),
            pltpu.VMEM((4, 2, SPAN, 512), f32),
            pltpu.VMEM((4, 2, 3, 64, 512), bf16),
            pltpu.VMEM((4, 2, 64, 512), bf16),
            pltpu.VMEM((SPAN, 1024), bf16),
            dma((2,)),
            dma((2, 3)),
            dma((2, 4)),
            dma((4,)),
            dma((2, 4)),
            dma((2, 4)),
            dma((3, 2, 2)),
            dma((3, 2, 2)),
            dma((4, 2, 3)),
            dma((4, 2, 3)),
            dma((4, 2)),
            dma((8,)),
        ],
        compiler_params=pltpu.CompilerParams(
            vmem_limit_bytes=56 * MIB, collective_id=0, has_side_effects=True
        ),
        name="layer",
    )(
        inner_input,
        state_input.reshape(SPAN, 512),
        step_input,
        decay_exponent[None, :],
        documents[None, :],
        filter_inner,
        filter_state.reshape(KERNEL, 512),
        norm_gain[None, :],
        skip_gain,
        gate_input,
        output_weight,
    )


def solution(mesh):
    placed = (
        P("seq", "head"),
        P("seq", None, "head"),
        P("seq", "head"),
        P("head", "seq"),
        P("head"),
        P("head"),
        P("seq"),
        P(None, "head"),
        P(None, None, "head"),
        P("head"),
        P("head", "seq"),
    )
    ways = dict(mesh.shape)
    fast = ways["seq"] == 8 and ways["head"] == 4
    return jax.shard_map(
        on_device_fast if fast else on_device, mesh=mesh, in_specs=placed, out_specs=P("seq", "head"), check_vma=False
    )
```

```python
import jax
import jax.numpy as jnp
from jax import lax
from jax.experimental import pallas as pl
from jax.experimental.pallas import tpu as pltpu
from jax.sharding import PartitionSpec as P

HEAD_DIM = 64
STATE = 128
GROUPS = 8
INNER = 8192
KERNEL = 4


highest = lax.Precision.HIGHEST


def entering(part, axis, combine, identity):
    place = lax.axis_index(axis)
    gathered = jax.tree.map(lambda a: lax.all_gather(a, axis), part)
    state = jax.tree.map(lambda a, e: jnp.zeros_like(a) + jnp.asarray(e, a.dtype), part, identity)

    def one(step, state):
        return combine(
            state, jax.tree.map(lambda a: lax.dynamic_index_in_dim(a, step, 0, False), gathered)
        )

    return lax.fori_loop(0, place, one, state)


def passed_along(value, axis, steps):
    count = lax.axis_size(axis)
    initial, last = (max(0, -steps), min(count, count - steps))
    return lax.ppermute(value, axis, [(source, source + steps) for source in range(initial, last)])


def causal_conv(extended, weights, segments_wide, segment_block):
    length = segment_block.shape[0]
    running = jnp.zeros(extended[:length].shape, jnp.float32)
    for offset in range(KERNEL):
        window = extended[offset : offset + length].astype(jnp.float32)
        matches = segments_wide[offset : offset + length] == segment_block
        matches = matches.reshape((length,) + (1,) * (extended.ndim - 1))
        running = running + jnp.where(matches, window * weights[offset], jnp.float32(0.0))
    return jax.nn.silu(running).astype(jnp.bfloat16)


def span_parts(values, write_rows, read_rows, step_size, decay_rate, segment_block, prior_segment):
    length = segment_block.shape[0]
    repeat = decay_rate.shape[0] // write_rows.shape[1]
    cumulative = jnp.cumsum(decay_rate, axis=1)
    places = jnp.arange(length)
    linked = (segment_block[:, None] == segment_block[None, :]) & (
        places[:, None] >= places[None, :]
    )
    spread = cumulative[:, :, None] - cumulative[:, None, :]
    decays = jnp.exp(jnp.where(linked[None], spread, -jnp.inf))
    scores = jnp.einsum("ign,jgn->gij", read_rows, write_rows, preferred_element_type=jnp.float32)
    scores = jnp.repeat(scores, repeat, axis=0)
    mixing = (decays * scores * step_size[:, None, :]).astype(jnp.bfloat16)
    within = jnp.einsum("hij,jhp->ihp", mixing, values, preferred_element_type=jnp.float32)
    inflow = jnp.exp(cumulative) * (segment_block == prior_segment)[None, :].astype(jnp.float32)
    final_segment = segment_block[-1]
    closing = (
        jnp.exp(cumulative[:, -1:] - cumulative)
        * (segment_block == final_segment)[None, :].astype(jnp.float32)
        * step_size
    )
    weighted = (values.astype(jnp.float32) * closing.T[:, :, None]).astype(jnp.bfloat16)
    writes = jnp.repeat(write_rows, repeat, axis=1)
    deposit = jnp.einsum("jhp,jhn->hpn", weighted, writes, preferred_element_type=jnp.float32)
    fading = jnp.exp(cumulative[:, -1]) * (final_segment == prior_segment).astype(jnp.float32)
    return (within, inflow, fading, deposit)


def reading(read_rows, held_state, repeat):
    readers = jnp.repeat(read_rows, repeat, axis=1).astype(jnp.float32)
    return jnp.einsum("ihn,hpn->ihp", readers, held_state, precision=highest)


def gated_norm(outputs, gates, norm_scale):
    height = outputs.shape[0]
    gated = outputs * jax.nn.silu(gates.astype(jnp.float32))
    grouped = gated.reshape(height, -1, INNER // GROUPS)
    mean_square = jnp.mean(grouped * grouped, axis=-1, keepdims=True)
    normed = (grouped * lax.rsqrt(mean_square + 1e-05)).reshape(height, -1) * norm_scale
    return normed.astype(jnp.bfloat16)


def chain_states(through, local_state):

    def combine_pair(earlier, later):
        return (earlier[0] * later[0], later[0][:, None, None] * earlier[1] + later[1])

    neutral = (jnp.ones_like(through), jnp.zeros_like(local_state))
    return entering((through, local_state), "seq", combine_pair, neutral)[1]


def on_device(
    inner_input,
    state_input,
    gate_input,
    step_input,
    decay_exponent,
    skip_gain,
    documents,
    filter_inner,
    filter_state,
    norm_gain,
    output_weight,
):
    margin = KERNEL - 1
    length = documents.shape[0]
    head_count = decay_exponent.shape[0]
    groups = state_input.shape[2] // STATE
    repeat = head_count // groups
    before_inner, before_state, before_segments = passed_along(
        (inner_input[-margin:], state_input[-margin:], documents[-margin:].astype(jnp.bfloat16)),
        "seq",
        1,
    )
    segments_wide = jnp.concatenate([before_segments.astype(jnp.int32), documents])
    inner_conv = causal_conv(
        jnp.concatenate([before_inner, inner_input]), filter_inner, segments_wide, documents
    )
    state_conv = causal_conv(
        jnp.concatenate([before_state, state_input]), filter_state, segments_wide, documents
    )
    values = inner_conv.reshape(length, head_count, HEAD_DIM)
    write_rows = state_conv[:, 0].reshape(length, groups, STATE)
    read_rows = state_conv[:, 1].reshape(length, groups, STATE)
    step_size = jax.nn.softplus(step_input)
    decay_rate = -step_size * jnp.exp(decay_exponent)[:, None]
    skipped = skip_gain[None, :, None] * values.astype(jnp.float32)
    prior_segment = segments_wide[margin - 1]
    pieces = [
        span_parts(values, write_rows, read_rows, step_size, decay_rate, documents, prior_segment)
    ]
    local_state = jnp.zeros((head_count, HEAD_DIM, STATE), jnp.float32)
    through = jnp.ones((head_count,), jnp.float32)
    block_index = 0
    within, inflow, fading, deposit = pieces[block_index]
    local_state = fading[:, None, None] * local_state + deposit
    through = through * fading
    carried = chain_states(through, local_state)
    block_index = 0
    within, inflow, fading, deposit = pieces[block_index]
    outputs = within + inflow.T[:, :, None] * reading(read_rows, carried, repeat) + skipped
    scan_out = outputs.reshape(length, head_count * HEAD_DIM)
    normed = gated_norm(scan_out, gate_input, norm_gain)
    partial_value = jnp.dot(
        normed,
        lax.all_gather(output_weight, "seq", axis=1, tiled=True),
        preferred_element_type=jnp.float32,
    )
    return lax.psum_scatter(partial_value, "head", scatter_dimension=1, tiled=True).astype(
        jnp.bfloat16
    )


MESH = pl.DeviceIdType.MESH
SPAN = 256
CHANNELS = 2048
HALF = 1024
MIB = 1 << 20


def fused_kernel(
    inner_ref,
    state_ref,
    step_ref,
    decay_ref,
    documents_ref,
    filter_inner_ref,
    filter_state_ref,
    gain_ref,
    skip_ref,
    gate_hbm,
    weight_hbm,
    out_ref,
    gate_ref,
    weight_ref,
    weight_in,
    halo_inner,
    halo_state,
    halo_documents,
    ext,
    conv,
    sconv,
    cum_rows,
    step_rows,
    in_rows,
    close_rows,
    weighted,
    part_ref,
    infl_ref,
    dep_ref,
    dep_stage,
    dep_in,
    fade_stage,
    fade_in,
    chain_out,
    chain_in,
    state_out,
    state_in,
    state_own,
    acts,
    partial,
    partial_own,
    sums_in,
    final_out,
    final_in,
    relay_in,
    local_sems,
    halo_sems,
    weight_sems,
    pair_sems,
    chain_sems,
    state_sems,
    act_send,
    act_recv,
    sum_send,
    sum_recv,
    final_send,
    final_recv,
    relay_send,
    relay_recv,
):
    s = lax.axis_index("seq")
    h = lax.axis_index("head")
    z, y = s // 2, s % 2
    me = s * 4 + h
    z_near = z + 1 - 2 * (z % 2)
    z_far = (z + 2) % 4
    y_pair = 2 * z + 1 - y
    z_pair = 2 * z_far + y

    def remote(src, dst, send, recv, seq, head=h):
        return pltpu.make_async_remote_copy(
            src_ref=src,
            dst_ref=dst,
            send_sem=send,
            recv_sem=recv,
            device_id=(seq, head),
            device_id_type=MESH,
        )

    gate_copy = pltpu.make_async_copy(gate_hbm, gate_ref, local_sems.at[0])
    weight_copy = pltpu.make_async_copy(weight_hbm, weight_ref, local_sems.at[1])
    gate_copy.start()
    weight_copy.start()

    barrier = pltpu.get_barrier_semaphore()

    @pl.loop(1, 32)
    def _(i):
        other = lax.rem(me + i, 32)
        pl.semaphore_signal(
            barrier, inc=1, device_id=(other // 4, other % 4), device_id_type=MESH
        )

    pl.semaphore_wait(barrier, 31)

    after = jnp.minimum(s + 1, 7)
    halo_copies = [
        remote(source, target, halo_sems.at[0, i], halo_sems.at[1, i], after)
        for i, (source, target) in enumerate(
            (
                (documents_ref, halo_documents),
                (state_ref.at[pl.ds(SPAN - 16, 16)], halo_state),
                (inner_ref.at[pl.ds(SPAN - 16, 16)], halo_inner),
            )
        )
    ]

    @pl.when(s < 7)
    def _():
        for copy in halo_copies:
            copy.start()

    weight_copies = []
    for i in range(8):
        rows = pl.ds(i * 256, 256)
        weight_copies.append(
            remote(
                weight_hbm.at[rows],
                weight_in.at[rows],
                weight_sems.at[0, i],
                weight_sems.at[1, i],
                2 * z_near + y,
            )
        )
    weight_copies[0].start()

    @pl.when(z > 0)
    def _():
        weight_copies[1].start()

    @pl.when(z % 2 == 1)
    def _():
        for copy in weight_copies[2:]:
            copy.start()

    @pl.when(s == 0)
    def _():
        halo_documents[...] = jnp.zeros_like(halo_documents)
        halo_state[...] = jnp.zeros_like(halo_state)
        halo_inner[...] = jnp.zeros_like(halo_inner)

    diagonal = lax.broadcasted_iota(jnp.int32, (32, 32), 0) == lax.broadcasted_iota(
        jnp.int32, (32, 32), 1
    )
    rate = jnp.sum(
        jnp.where(diagonal, jnp.broadcast_to(jnp.exp(decay_ref[...]), (32, 32)), 0.0),
        axis=1,
        keepdims=True,
    )
    value = step_ref[...]
    step = jnp.maximum(value, 0.0) + jnp.log1p(jnp.exp(-jnp.abs(value)))
    row_at = lax.broadcasted_iota(jnp.int32, (SPAN, SPAN), 0)
    col_at = lax.broadcasted_iota(jnp.int32, (SPAN, SPAN), 1)
    upper = (row_at <= col_at).astype(jnp.float32)
    cumulative = jnp.dot(
        -step * rate, upper, precision=highest, preferred_element_type=jnp.float32
    )
    documents = documents_ref[...].astype(jnp.float32)
    final = (documents == documents[:, SPAN - 1 :]).astype(jnp.float32)
    step_rows[...] = step
    cum_rows[...] = cumulative
    close_rows[...] = jnp.exp(cumulative[:, SPAN - 1 :] - cumulative) * final * step

    @pl.when(s > 0)
    def _():
        for copy in halo_copies:
            copy.wait_recv()

    before = halo_documents[...].astype(jnp.float32)
    in_rows[...] = jnp.exp(cumulative) * (documents == before[:, SPAN - 1 :]).astype(jnp.float32)
    lane = lax.broadcasted_iota(jnp.int32, (8, SPAN), 1)
    mark_row = lax.broadcasted_iota(jnp.int32, (8, SPAN), 0)
    documents_8 = jnp.broadcast_to(documents, (8, SPAN))
    before_8 = jnp.broadcast_to(before, (8, SPAN))
    mark_rows = documents_8
    for k in (1, 2, 3):
        shifted = jnp.where(
            lane < k, pltpu.roll(before_8, k, axis=1), pltpu.roll(documents_8, k, axis=1)
        )
        same = (shifted == documents_8).astype(jnp.float32)
        mark_rows = jnp.where(mark_row == k, same, mark_rows)
    marks = mark_rows.T

    def convolve(source, halo, at, taps, target):
        lanes = pl.ds(at, 256)
        ext[0:16, :] = halo[:, lanes].astype(jnp.float32)
        ext[16:272, :] = source[:, lanes].astype(jnp.float32)
        running = marks[:, 3:4] * (ext[13:269, :] * taps[0:1, lanes])
        running = running + marks[:, 2:3] * (ext[14:270, :] * taps[1:2, lanes])
        running = running + marks[:, 1:2] * (ext[15:271, :] * taps[2:3, lanes])
        running = running + ext[16:272, :] * taps[3:4, lanes]
        target[:, lanes] = (running * jax.nn.sigmoid(running)).astype(jnp.bfloat16)

    @pl.loop(0, 2)
    def _(i):
        convolve(state_ref, halo_state, pl.multiple_of(i * 256, 256), filter_state_ref, sconv)

    linked = (marks[:, 0:1] == documents) & (row_at >= col_at)
    low = lax.broadcasted_iota(jnp.int32, (SPAN, 128), 1) < HEAD_DIM

    apart = pl.ds(pl.multiple_of((1 - y) * HALF, HALF), HALF)
    send_dep = remote(dep_stage, dep_in, pair_sems.at[0], pair_sems.at[1], y_pair)
    send_fade = remote(fade_stage, fade_in, pair_sems.at[2], pair_sems.at[3], y_pair)

    @pl.loop(0, 2)
    def _(turn):
        group = jnp.where(turn == 0, 1 - y, y)
        base = group * HALF

        @pl.loop(0, 4)
        def _(i):
            at = pl.multiple_of(base + i * 256, 256)
            convolve(inner_ref, halo_inner, at, filter_inner_ref, conv)

        writes = sconv[:, pl.ds(pl.multiple_of(group * 128, 128), 128)]
        heads = pl.ds(pl.multiple_of(group * 16, 16), 16)
        in_cols = in_rows[heads, :].T
        close_cols = close_rows[heads, :].T
        for pair in range(8):
            first = pair * 2
            at = pl.ds(pl.multiple_of(base + pair * 128, 128), 128)

            def both(cols):
                return jnp.where(low, cols[:, first : first + 1], cols[:, first + 1 : first + 2])

            weighted[:, pair * 128 : pair * 128 + 128] = (
                conv[:, at].astype(jnp.float32) * both(close_cols)
            ).astype(jnp.bfloat16)
            infl_ref[:, at] = both(in_cols)
        dep_ref[...] = lax.dot_general(
            writes, weighted[...], (((0,), (0,)), ((), ())), preferred_element_type=jnp.float32
        )

        @pl.when(turn == 0)
        def _():
            dep_stage[...] = dep_ref[...].astype(jnp.bfloat16)
            fade_stage[...] = infl_ref[SPAN - 8 : SPAN, apart]
            send_fade.start()
            send_dep.start()

    def mixing_of(group):
        base = group * HALF
        writes = sconv[:, pl.ds(pl.multiple_of(group * 128, 128), 128)]
        reads = sconv[:, pl.ds(pl.multiple_of(256 + group * 128, 128), 128)]
        scores = lax.dot_general(
            reads, writes, (((1,), (1,)), ((), ())), preferred_element_type=jnp.float32
        )
        scores = jnp.where(linked, scores, 0.0)
        heads = pl.ds(pl.multiple_of(group * 16, 16), 16)
        cums = cum_rows[heads, :]
        steps = step_rows[heads, :]
        cum_cols = cums.T
        for pair in range(8):
            first = pair * 2
            at = pl.ds(pl.multiple_of(base + pair * 128, 128), 128)
            x = conv[:, at]

            def mixed(j):
                spread = jnp.minimum(cum_cols[:, j : j + 1] - cums[j : j + 1, :], 0.0)
                mixing = (jnp.exp(spread) * scores * steps[j : j + 1, :]).astype(jnp.bfloat16)
                return jnp.dot(mixing, x, preferred_element_type=jnp.float32)

            gain = jnp.where(low, skip_ref[group * 16 + first], skip_ref[group * 16 + first + 1])
            part_ref[:, at] = jnp.where(low, mixed(first), mixed(first + 1)) + gain * x.astype(
                jnp.float32
            )

    @pl.when(z == 0)
    def _():
        chain_in[...] = jnp.zeros_like(chain_in)

    is_first = y == 0
    chain_copies = [
        remote(
            chain_out.at[q],
            chain_in.at[q],
            chain_sems.at[0, q],
            chain_sems.at[1, q],
            jnp.minimum(s + 2, 7),
        )
        for q in range(4)
    ]
    state_copies = [
        remote(state_out.at[q], state_in.at[q], state_sems.at[0, q], state_sems.at[1, q], y_pair)
        for q in range(4)
    ]
    def chain():
        send_fade.wait_recv()
        send_dep.wait_recv()
        for q in range(4):
            lanes = pl.ds(pl.multiple_of(y * HALF + q * 256, 256), 256)
            here = slice(q * 256, q * 256 + 256)
            dep_own = dep_ref[:, here]
            dep_other = dep_in[:, here].astype(jnp.float32)
            fade_own = infl_ref[SPAN - 8 : SPAN, lanes][7:8]
            fade_other = fade_in[7:8, here]
            dep_0 = jnp.where(is_first, dep_own, dep_other)
            dep_1 = jnp.where(is_first, dep_other, dep_own)
            fade_0 = jnp.where(is_first, fade_own, fade_other)
            fade_1 = jnp.where(is_first, fade_other, fade_own)
            slab = fade_1 * dep_0 + dep_1
            slab_fade = fade_0 * fade_1

            @pl.when(z > 0)
            def _():
                chain_copies[q].wait_recv()

            entering_0 = chain_in[q].astype(jnp.float32)
            chain_out[q] = (slab_fade * entering_0 + slab).astype(jnp.bfloat16)

            @pl.when(z < 3)
            def _():
                chain_copies[q].start()

            entering_1 = fade_0 * entering_0 + dep_0
            state_own[:, here] = jnp.where(is_first, entering_0, entering_1).astype(jnp.bfloat16)
            state_out[q] = jnp.where(is_first, entering_1, entering_0).astype(jnp.bfloat16)
            state_copies[q].start()

    @pl.loop(0, 3)
    def _(phase):
        late = jnp.where(z >= 2, 1, 0)

        @pl.when(phase != 1 + late)
        def _():
            mixing_of(jnp.where(phase == 0, 1 - y, y))

        @pl.when(phase == 1 + late)
        def _():
            chain()

    @pl.when(z == 0)
    def _():
        weight_copies[1].start()

    @pl.when(z % 2 == 0)
    def _():
        for copy in weight_copies[2:]:
            copy.start()

    gate_copy.wait()

    def act_copy(slot, half, quarter):
        source = 2 if slot == 3 else 0
        rows = pl.ds(quarter * 128, 128)
        return remote(
            acts.at[source, half, rows],
            acts.at[slot, half, rows],
            act_send.at[slot - 1, half, quarter],
            act_recv.at[slot - 1, half, quarter],
            z_pair if slot == 2 else y_pair,
        )

    def norm_half(half, state):
        lanes = pl.ds(pl.multiple_of(half * HALF, HALF), HALF)
        reads_at = pl.ds(pl.multiple_of(256 + half * 128, 128), 128)
        for quarter in range(2):

            @pl.loop(0, 2)
            def _(i):
                rows = pl.ds(pl.multiple_of(quarter * 128 + i * 64, 64), 64)
                read = jnp.dot(sconv[rows, reads_at], state, preferred_element_type=jnp.float32)
                gate = gate_ref[rows, lanes].astype(jnp.float32)
                scan = part_ref[rows, lanes] + infl_ref[rows, lanes] * read
                gated = scan * (gate * jax.nn.sigmoid(gate))
                mean = jnp.sum(gated * gated, axis=1, keepdims=True) * (1.0 / HALF)
                normed = gated * lax.rsqrt(mean + 1e-05) * gain_ref[:, lanes]
                acts[0, half, rows, :] = normed.astype(jnp.bfloat16)

            act_copy(2, half, quarter).start()
            act_copy(1, half, quarter).start()

    norm_half(y, state_own[...])
    for q in range(4):
        state_copies[q].wait_recv()
    norm_half(1 - y, jnp.concatenate([state_in[q] for q in range(4)], axis=1))

    def sum_copy(k, side, o):
        to = h ^ o
        rows = pl.ds(pl.multiple_of(to * 64, 64), 64)
        return remote(
            partial.at[k, side, rows],
            sums_in.at[k, side, o - 1],
            sum_send.at[k, side, o - 1],
            sum_recv.at[k, side, o - 1],
            s,
            to,
        )

    def project(k, side):
        weight = (weight_ref, weight_in)[side]

        @pl.loop(0, 2)
        def _(i):
            lanes = pl.ds(pl.multiple_of(i * 256, 256), 256)
            total = jnp.dot(
                acts[k, 0], weight[0:HALF, lanes], preferred_element_type=jnp.float32
            ) + jnp.dot(
                acts[k, 1], weight[HALF:CHANNELS, lanes], preferred_element_type=jnp.float32
            )
            partial_own[k, side, :, lanes] = total
            partial[k, side, :, lanes] = total.astype(jnp.bfloat16)

        for o in (2, 3, 1):
            sum_copy(k, side, o).start()

    rows_own = pl.ds(pl.multiple_of(h * 64, 64), 64)
    spot_own = pl.ds(pl.multiple_of(y * 512, 512), 512)

    def final_copy(source, k, side, target, head):
        return remote(
            source,
            final_in.at[rows_own, spot_own],
            final_send.at[k, side],
            final_recv.at[y * 4 + h],
            target,
            head,
        )

    def hand_over(k, side, source):
        z_of = z if k < 2 else z_far
        head = z_of if side == 0 else z_of + 1 - 2 * (z_of % 2)
        copy = final_copy(source, k, side, s if k % 2 == 0 else y_pair, head)
        return copy, (head == h if k % 2 == 0 else None)

    def deliver(k, side, source):
        copy, stays = hand_over(k, side, source)
        if stays is None:
            copy.start()
            return

        @pl.when(stays)
        def _():
            final_in[rows_own, spot_own] = source[...]

        @pl.when(jnp.logical_not(stays))
        def _():
            copy.start()

    def relay_copy(k, side):
        return remote(
            final_out.at[k, side],
            relay_in.at[k - 2, side],
            relay_send.at[k - 2, side],
            relay_recv.at[k - 2, side],
            z_pair,
        )

    def pass_on(k, side):
        relay_copy(k, side).wait_recv()
        deliver(k, side, relay_in.at[k - 2, side])

    def finish(k, side):
        for o in (1, 2, 3):
            sum_copy(k, side, o).wait_recv()
        total = partial_own[k, side, rows_own, :]
        for o in range(3):
            total = total + sums_in[k, side, o].astype(jnp.float32)
        final_out[k, side] = total.astype(jnp.bfloat16)
        if k < 2:
            deliver(k, side, final_out.at[k, side])
        else:
            relay_copy(k, side).start()

    def arrived(slot, half):
        for quarter in range(2):
            act_copy(slot, half, quarter).wait_recv()
            if slot == 2:
                act_copy(3, half, quarter).start()

    weight_copy.wait()
    project(0, 0)
    arrived(1, 1 - y)
    arrived(1, y)
    project(1, 0)
    finish(0, 0)
    arrived(2, y)
    for copy in weight_copies:
        copy.wait_recv()
    project(0, 1)
    finish(1, 0)
    project(1, 1)
    finish(0, 1)
    arrived(2, 1 - y)
    project(2, 0)
    finish(1, 1)
    project(2, 1)
    finish(2, 0)
    arrived(3, 1 - y)
    arrived(3, y)
    project(3, 0)
    finish(2, 1)
    project(3, 1)
    finish(3, 0)
    finish(3, 1)
    for k in (2, 3):
        for side in range(2):
            pass_on(k, side)

    z_from = 2 * (h // 2) + z % 2
    for y_from in range(2):
        for h_from in range(4):
            rows = slice(h_from * 64, h_from * 64 + 64)
            spot = slice(y_from * 512, y_from * 512 + 512)
            mine = (y_from == y) & (h_from == h)

            @pl.when(jnp.logical_not(mine))
            def _():
                remote(
                    final_out.at[0, 0],
                    final_in.at[rows, spot],
                    final_send.at[0, 0],
                    final_recv.at[y_from * 4 + h_from],
                    2 * z_from + y_from,
                    h_from,
                ).wait_recv()

    out_ref[...] = final_in[...]

    @pl.when(s < 7)
    def _():
        for copy in halo_copies:
            copy.wait_send()

    send_dep.wait_send()
    send_fade.wait_send()
    for copy in weight_copies:
        copy.wait_send()
    for q in range(4):
        state_copies[q].wait_send()

        @pl.when(z < 3)
        def _():
            chain_copies[q].wait_send()

    for slot in (1, 2, 3):
        for half in range(2):
            for quarter in range(2):
                act_copy(slot, half, quarter).wait_send()
    for k in range(4):
        for side in range(2):
            for o in (1, 2, 3):
                sum_copy(k, side, o).wait_send()
            if k >= 2:
                relay_copy(k, side).wait_send()
            source = final_out.at[k, side] if k < 2 else relay_in.at[k - 2, side]
            copy, stays = hand_over(k, side, source)
            if stays is None:
                copy.wait_send()
            else:

                @pl.when(jnp.logical_not(stays))
                def _():
                    copy.wait_send()


def on_device_fast(
    inner_input,
    state_input,
    gate_input,
    step_input,
    decay_exponent,
    skip_gain,
    documents,
    filter_inner,
    filter_state,
    norm_gain,
    output_weight,
):
    vmem = pl.BlockSpec(memory_space=pltpu.VMEM)
    smem = pl.BlockSpec(memory_space=pltpu.SMEM)
    anywhere = pl.BlockSpec(memory_space=pl.ANY)
    bf16, f32 = jnp.bfloat16, jnp.float32
    dma = pltpu.SemaphoreType.DMA
    return pl.pallas_call(
        fused_kernel,
        out_shape=jax.ShapeDtypeStruct((SPAN, 1024), bf16),
        in_specs=[vmem] * 8 + [smem] + [anywhere] * 2,
        out_specs=vmem,
        scratch_shapes=[
            pltpu.VMEM((SPAN, CHANNELS), bf16),
            pltpu.VMEM((CHANNELS, 512), bf16),
            pltpu.VMEM((CHANNELS, 512), bf16),
            pltpu.VMEM((16, CHANNELS), bf16),
            pltpu.VMEM((16, 512), bf16),
            pltpu.VMEM((1, SPAN), jnp.int32),
            pltpu.VMEM((SPAN + 16, 256), f32),
            pltpu.VMEM((SPAN, CHANNELS), bf16),
            pltpu.VMEM((SPAN, 512), bf16),
            pltpu.VMEM((32, SPAN), f32),
            pltpu.VMEM((32, SPAN), f32),
            pltpu.VMEM((32, SPAN), f32),
            pltpu.VMEM((32, SPAN), f32),
            pltpu.VMEM((SPAN, HALF), bf16),
            pltpu.VMEM((SPAN, CHANNELS), f32),
            pltpu.VMEM((SPAN, CHANNELS), f32),
            pltpu.VMEM((STATE, HALF), f32),
            pltpu.VMEM((STATE, HALF), bf16),
            pltpu.VMEM((STATE, HALF), bf16),
            pltpu.VMEM((8, HALF), f32),
            pltpu.VMEM((8, HALF), f32),
            pltpu.VMEM((4, STATE, 256), bf16),
            pltpu.VMEM((4, STATE, 256), bf16),
            pltpu.VMEM((4, STATE, 256), bf16),
            pltpu.VMEM((4, STATE, 256), bf16),
            pltpu.VMEM((STATE, HALF), bf16),
            pltpu.VMEM((4, 2, SPAN, HALF), bf16),
            pltpu.VMEM((4, 2, SPAN, 512), bf16),
            pltpu.VMEM((4, 2, SPAN, 512), f32),
            pltpu.VMEM((4, 2, 3, 64, 512), bf16),
            pltpu.VMEM((4, 2, 64, 512), bf16),
            pltpu.VMEM((SPAN, 1024), bf16),
            pltpu.VMEM((2, 2, 64, 512), bf16),
            dma((2,)),
            dma((2, 3)),
            dma((2, 8)),
            dma((4,)),
            dma((2, 4)),
            dma((2, 4)),
            dma((3, 2, 2)),
            dma((3, 2, 2)),
            dma((4, 2, 3)),
            dma((4, 2, 3)),
            dma((4, 2)),
            dma((8,)),
            dma((2, 2)),
            dma((2, 2)),
        ],
        compiler_params=pltpu.CompilerParams(
            vmem_limit_bytes=56 * MIB, collective_id=0, has_side_effects=True
        ),
        name="layer",
    )(
        inner_input,
        state_input.reshape(SPAN, 512),
        step_input,
        decay_exponent[None, :],
        documents[None, :],
        filter_inner,
        filter_state.reshape(KERNEL, 512),
        norm_gain[None, :],
        skip_gain,
        gate_input,
        output_weight,
    )


def solution(mesh):
    placed = (
        P("seq", "head"),
        P("seq", None, "head"),
        P("seq", "head"),
        P("head", "seq"),
        P("head"),
        P("head"),
        P("seq"),
        P(None, "head"),
        P(None, None, "head"),
        P("head"),
        P("head", "seq"),
    )
    ways = dict(mesh.shape)
    fast = ways["seq"] == 8 and ways["head"] == 4
    return jax.shard_map(
        on_device_fast if fast else on_device, mesh=mesh, in_specs=placed, out_specs=P("seq", "head"), check_vma=False
    )
```

```python
import jax
import jax.numpy as jnp
from jax import lax
from jax.experimental import pallas as pl
from jax.experimental.pallas import tpu as pltpu
from jax.sharding import PartitionSpec as P

HEAD_DIM = 64
STATE = 128
GROUPS = 8
INNER = 8192
KERNEL = 4


highest = lax.Precision.HIGHEST


def entering(part, axis, combine, identity):
    place = lax.axis_index(axis)
    gathered = jax.tree.map(lambda a: lax.all_gather(a, axis), part)
    state = jax.tree.map(lambda a, e: jnp.zeros_like(a) + jnp.asarray(e, a.dtype), part, identity)

    def one(step, state):
        return combine(
            state, jax.tree.map(lambda a: lax.dynamic_index_in_dim(a, step, 0, False), gathered)
        )

    return lax.fori_loop(0, place, one, state)


def passed_along(value, axis, steps):
    count = lax.axis_size(axis)
    initial, last = (max(0, -steps), min(count, count - steps))
    return lax.ppermute(value, axis, [(source, source + steps) for source in range(initial, last)])


def causal_conv(extended, weights, segments_wide, segment_block):
    length = segment_block.shape[0]
    running = jnp.zeros(extended[:length].shape, jnp.float32)
    for offset in range(KERNEL):
        window = extended[offset : offset + length].astype(jnp.float32)
        matches = segments_wide[offset : offset + length] == segment_block
        matches = matches.reshape((length,) + (1,) * (extended.ndim - 1))
        running = running + jnp.where(matches, window * weights[offset], jnp.float32(0.0))
    return jax.nn.silu(running).astype(jnp.bfloat16)


def span_parts(values, write_rows, read_rows, step_size, decay_rate, segment_block, prior_segment):
    length = segment_block.shape[0]
    repeat = decay_rate.shape[0] // write_rows.shape[1]
    cumulative = jnp.cumsum(decay_rate, axis=1)
    places = jnp.arange(length)
    linked = (segment_block[:, None] == segment_block[None, :]) & (
        places[:, None] >= places[None, :]
    )
    spread = cumulative[:, :, None] - cumulative[:, None, :]
    decays = jnp.exp(jnp.where(linked[None], spread, -jnp.inf))
    scores = jnp.einsum("ign,jgn->gij", read_rows, write_rows, preferred_element_type=jnp.float32)
    scores = jnp.repeat(scores, repeat, axis=0)
    mixing = (decays * scores * step_size[:, None, :]).astype(jnp.bfloat16)
    within = jnp.einsum("hij,jhp->ihp", mixing, values, preferred_element_type=jnp.float32)
    inflow = jnp.exp(cumulative) * (segment_block == prior_segment)[None, :].astype(jnp.float32)
    final_segment = segment_block[-1]
    closing = (
        jnp.exp(cumulative[:, -1:] - cumulative)
        * (segment_block == final_segment)[None, :].astype(jnp.float32)
        * step_size
    )
    weighted = (values.astype(jnp.float32) * closing.T[:, :, None]).astype(jnp.bfloat16)
    writes = jnp.repeat(write_rows, repeat, axis=1)
    deposit = jnp.einsum("jhp,jhn->hpn", weighted, writes, preferred_element_type=jnp.float32)
    fading = jnp.exp(cumulative[:, -1]) * (final_segment == prior_segment).astype(jnp.float32)
    return (within, inflow, fading, deposit)


def reading(read_rows, held_state, repeat):
    readers = jnp.repeat(read_rows, repeat, axis=1).astype(jnp.float32)
    return jnp.einsum("ihn,hpn->ihp", readers, held_state, precision=highest)


def gated_norm(outputs, gates, norm_scale):
    height = outputs.shape[0]
    gated = outputs * jax.nn.silu(gates.astype(jnp.float32))
    grouped = gated.reshape(height, -1, INNER // GROUPS)
    mean_square = jnp.mean(grouped * grouped, axis=-1, keepdims=True)
    normed = (grouped * lax.rsqrt(mean_square + 1e-05)).reshape(height, -1) * norm_scale
    return normed.astype(jnp.bfloat16)


def chain_states(through, local_state):

    def combine_pair(earlier, later):
        return (earlier[0] * later[0], later[0][:, None, None] * earlier[1] + later[1])

    neutral = (jnp.ones_like(through), jnp.zeros_like(local_state))
    return entering((through, local_state), "seq", combine_pair, neutral)[1]


def on_device(
    inner_input,
    state_input,
    gate_input,
    step_input,
    decay_exponent,
    skip_gain,
    documents,
    filter_inner,
    filter_state,
    norm_gain,
    output_weight,
):
    margin = KERNEL - 1
    length = documents.shape[0]
    head_count = decay_exponent.shape[0]
    groups = state_input.shape[2] // STATE
    repeat = head_count // groups
    before_inner, before_state, before_segments = passed_along(
        (inner_input[-margin:], state_input[-margin:], documents[-margin:].astype(jnp.bfloat16)),
        "seq",
        1,
    )
    segments_wide = jnp.concatenate([before_segments.astype(jnp.int32), documents])
    inner_conv = causal_conv(
        jnp.concatenate([before_inner, inner_input]), filter_inner, segments_wide, documents
    )
    state_conv = causal_conv(
        jnp.concatenate([before_state, state_input]), filter_state, segments_wide, documents
    )
    values = inner_conv.reshape(length, head_count, HEAD_DIM)
    write_rows = state_conv[:, 0].reshape(length, groups, STATE)
    read_rows = state_conv[:, 1].reshape(length, groups, STATE)
    step_size = jax.nn.softplus(step_input)
    decay_rate = -step_size * jnp.exp(decay_exponent)[:, None]
    skipped = skip_gain[None, :, None] * values.astype(jnp.float32)
    prior_segment = segments_wide[margin - 1]
    pieces = [
        span_parts(values, write_rows, read_rows, step_size, decay_rate, documents, prior_segment)
    ]
    local_state = jnp.zeros((head_count, HEAD_DIM, STATE), jnp.float32)
    through = jnp.ones((head_count,), jnp.float32)
    block_index = 0
    within, inflow, fading, deposit = pieces[block_index]
    local_state = fading[:, None, None] * local_state + deposit
    through = through * fading
    carried = chain_states(through, local_state)
    block_index = 0
    within, inflow, fading, deposit = pieces[block_index]
    outputs = within + inflow.T[:, :, None] * reading(read_rows, carried, repeat) + skipped
    scan_out = outputs.reshape(length, head_count * HEAD_DIM)
    normed = gated_norm(scan_out, gate_input, norm_gain)
    partial_value = jnp.dot(
        normed,
        lax.all_gather(output_weight, "seq", axis=1, tiled=True),
        preferred_element_type=jnp.float32,
    )
    return lax.psum_scatter(partial_value, "head", scatter_dimension=1, tiled=True).astype(
        jnp.bfloat16
    )


MESH = pl.DeviceIdType.MESH
SPAN = 256
CHANNELS = 2048
HALF = 1024
MIB = 1 << 20


def fused_kernel(
    inner_ref,
    state_ref,
    step_ref,
    decay_ref,
    documents_ref,
    filter_inner_ref,
    filter_state_ref,
    gain_ref,
    skip_ref,
    gate_hbm,
    weight_hbm,
    out_ref,
    gate_ref,
    weight_ref,
    weight_in,
    halo_inner,
    halo_state,
    halo_documents,
    ext,
    conv,
    sconv,
    cum_rows,
    step_rows,
    in_rows,
    close_rows,
    weighted,
    part_ref,
    infl_ref,
    dep_ref,
    dep_stage,
    dep_in,
    fade_stage,
    fade_in,
    chain_out,
    chain_in,
    state_out,
    state_in,
    state_own,
    acts,
    partial,
    partial_own,
    sums_in,
    final_out,
    final_in,
    local_sems,
    halo_sems,
    weight_sems,
    pair_sems,
    chain_sems,
    state_sems,
    act_send,
    act_recv,
    sum_send,
    sum_recv,
    final_send,
    final_recv,
):
    s = lax.axis_index("seq")
    h = lax.axis_index("head")
    z, y = s // 2, s % 2
    me = s * 4 + h
    z_near = z + 1 - 2 * (z % 2)
    z_far = (z + 2) % 4
    y_pair = 2 * z + 1 - y
    z_pair = 2 * z_far + y

    def remote(src, dst, send, recv, seq, head=h):
        return pltpu.make_async_remote_copy(
            src_ref=src,
            dst_ref=dst,
            send_sem=send,
            recv_sem=recv,
            device_id=(seq, head),
            device_id_type=MESH,
        )

    gate_copy = pltpu.make_async_copy(gate_hbm, gate_ref, local_sems.at[0])
    weight_copy = pltpu.make_async_copy(weight_hbm, weight_ref, local_sems.at[1])
    gate_copy.start()
    weight_copy.start()

    barrier = pltpu.get_barrier_semaphore()

    @pl.loop(1, 32)
    def _(i):
        other = lax.rem(me + i, 32)
        pl.semaphore_signal(
            barrier, inc=1, device_id=(other // 4, other % 4), device_id_type=MESH
        )

    pl.semaphore_wait(barrier, 31)

    after = jnp.minimum(s + 1, 7)
    halo_copies = [
        remote(source, target, halo_sems.at[0, i], halo_sems.at[1, i], after)
        for i, (source, target) in enumerate(
            (
                (documents_ref, halo_documents),
                (state_ref.at[pl.ds(SPAN - 16, 16)], halo_state),
                (inner_ref.at[pl.ds(SPAN - 16, 16)], halo_inner),
            )
        )
    ]

    @pl.when(s < 7)
    def _():
        for copy in halo_copies:
            copy.start()

    weight_copies = []
    for i in range(8):
        rows = pl.ds(i * 256, 256)
        weight_copies.append(
            remote(
                weight_hbm.at[rows],
                weight_in.at[rows],
                weight_sems.at[0, i],
                weight_sems.at[1, i],
                2 * z_near + y,
            )
        )
    weight_copies[0].start()

    @pl.when(z > 0)
    def _():
        weight_copies[1].start()
        weight_copies[2].start()

    @pl.when(z % 2 == 1)
    def _():
        for copy in weight_copies[3:]:
            copy.start()

    @pl.when(s == 0)
    def _():
        halo_documents[...] = jnp.zeros_like(halo_documents)
        halo_state[...] = jnp.zeros_like(halo_state)
        halo_inner[...] = jnp.zeros_like(halo_inner)

    diagonal = lax.broadcasted_iota(jnp.int32, (32, 32), 0) == lax.broadcasted_iota(
        jnp.int32, (32, 32), 1
    )
    rate = jnp.sum(
        jnp.where(diagonal, jnp.broadcast_to(jnp.exp(decay_ref[...]), (32, 32)), 0.0),
        axis=1,
        keepdims=True,
    )
    value = step_ref[...]
    step = jnp.maximum(value, 0.0) + jnp.log1p(jnp.exp(-jnp.abs(value)))
    row_at = lax.broadcasted_iota(jnp.int32, (SPAN, SPAN), 0)
    col_at = lax.broadcasted_iota(jnp.int32, (SPAN, SPAN), 1)
    upper = (row_at <= col_at).astype(jnp.float32)
    cumulative = jnp.dot(
        -step * rate, upper, precision=highest, preferred_element_type=jnp.float32
    )
    documents = documents_ref[...].astype(jnp.float32)
    final = (documents == documents[:, SPAN - 1 :]).astype(jnp.float32)
    step_rows[...] = step
    cum_rows[...] = cumulative
    close_rows[...] = jnp.exp(cumulative[:, SPAN - 1 :] - cumulative) * final * step

    @pl.when(s > 0)
    def _():
        for copy in halo_copies:
            copy.wait_recv()

    before = halo_documents[...].astype(jnp.float32)
    in_rows[...] = jnp.exp(cumulative) * (documents == before[:, SPAN - 1 :]).astype(jnp.float32)
    lane = lax.broadcasted_iota(jnp.int32, (8, SPAN), 1)
    mark_row = lax.broadcasted_iota(jnp.int32, (8, SPAN), 0)
    documents_8 = jnp.broadcast_to(documents, (8, SPAN))
    before_8 = jnp.broadcast_to(before, (8, SPAN))
    mark_rows = documents_8
    for k in (1, 2, 3):
        shifted = jnp.where(
            lane < k, pltpu.roll(before_8, k, axis=1), pltpu.roll(documents_8, k, axis=1)
        )
        same = (shifted == documents_8).astype(jnp.float32)
        mark_rows = jnp.where(mark_row == k, same, mark_rows)
    marks = mark_rows.T

    def convolve(source, halo, at, taps, target):
        lanes = pl.ds(at, 256)
        ext[0:16, :] = halo[:, lanes].astype(jnp.float32)
        ext[16:272, :] = source[:, lanes].astype(jnp.float32)
        running = marks[:, 3:4] * (ext[13:269, :] * taps[0:1, lanes])
        running = running + marks[:, 2:3] * (ext[14:270, :] * taps[1:2, lanes])
        running = running + marks[:, 1:2] * (ext[15:271, :] * taps[2:3, lanes])
        running = running + ext[16:272, :] * taps[3:4, lanes]
        target[:, lanes] = (running * jax.nn.sigmoid(running)).astype(jnp.bfloat16)

    @pl.loop(0, 2)
    def _(i):
        convolve(state_ref, halo_state, pl.multiple_of(i * 256, 256), filter_state_ref, sconv)

    linked = (marks[:, 0:1] == documents) & (row_at >= col_at)
    low = lax.broadcasted_iota(jnp.int32, (SPAN, 128), 1) < HEAD_DIM

    apart = pl.ds(pl.multiple_of((1 - y) * HALF, HALF), HALF)
    send_dep = remote(dep_stage, dep_in, pair_sems.at[0], pair_sems.at[1], y_pair)
    send_fade = remote(fade_stage, fade_in, pair_sems.at[2], pair_sems.at[3], y_pair)

    @pl.loop(0, 2)
    def _(turn):
        group = jnp.where(turn == 0, 1 - y, y)
        base = group * HALF

        @pl.loop(0, 4)
        def _(i):
            at = pl.multiple_of(base + i * 256, 256)
            convolve(inner_ref, halo_inner, at, filter_inner_ref, conv)

        writes = sconv[:, pl.ds(pl.multiple_of(group * 128, 128), 128)]
        heads = pl.ds(pl.multiple_of(group * 16, 16), 16)
        in_cols = in_rows[heads, :].T
        close_cols = close_rows[heads, :].T
        for pair in range(8):
            first = pair * 2
            at = pl.ds(pl.multiple_of(base + pair * 128, 128), 128)

            def both(cols):
                return jnp.where(low, cols[:, first : first + 1], cols[:, first + 1 : first + 2])

            weighted[:, pair * 128 : pair * 128 + 128] = (
                conv[:, at].astype(jnp.float32) * both(close_cols)
            ).astype(jnp.bfloat16)
            infl_ref[:, at] = both(in_cols)
        dep_ref[...] = lax.dot_general(
            writes, weighted[...], (((0,), (0,)), ((), ())), preferred_element_type=jnp.float32
        )

        @pl.when(turn == 0)
        def _():
            dep_stage[...] = dep_ref[...].astype(jnp.bfloat16)
            fade_stage[...] = infl_ref[SPAN - 8 : SPAN, apart]
            send_fade.start()
            send_dep.start()

    def mixing_of(group):
        base = group * HALF
        writes = sconv[:, pl.ds(pl.multiple_of(group * 128, 128), 128)]
        reads = sconv[:, pl.ds(pl.multiple_of(256 + group * 128, 128), 128)]
        scores = lax.dot_general(
            reads, writes, (((1,), (1,)), ((), ())), preferred_element_type=jnp.float32
        )
        scores = jnp.where(linked, scores, 0.0)
        heads = pl.ds(pl.multiple_of(group * 16, 16), 16)
        cums = cum_rows[heads, :]
        steps = step_rows[heads, :]
        cum_cols = cums.T
        for pair in range(8):
            first = pair * 2
            at = pl.ds(pl.multiple_of(base + pair * 128, 128), 128)
            x = conv[:, at]

            def mixed(j):
                spread = jnp.minimum(cum_cols[:, j : j + 1] - cums[j : j + 1, :], 0.0)
                mixing = (jnp.exp(spread) * scores * steps[j : j + 1, :]).astype(jnp.bfloat16)
                return jnp.dot(mixing, x, preferred_element_type=jnp.float32)

            gain = jnp.where(low, skip_ref[group * 16 + first], skip_ref[group * 16 + first + 1])
            part_ref[:, at] = jnp.where(low, mixed(first), mixed(first + 1)) + gain * x.astype(
                jnp.float32
            )

    @pl.when(z == 0)
    def _():
        chain_in[...] = jnp.zeros_like(chain_in)

    is_first = y == 0
    chain_copies = [
        remote(
            chain_out.at[q],
            chain_in.at[q],
            chain_sems.at[0, q],
            chain_sems.at[1, q],
            jnp.minimum(s + 2, 7),
        )
        for q in range(4)
    ]
    state_copies = [
        remote(state_out.at[q], state_in.at[q], state_sems.at[0, q], state_sems.at[1, q], y_pair)
        for q in range(4)
    ]
    def chain():
        send_fade.wait_recv()
        send_dep.wait_recv()
        for q in range(4):
            lanes = pl.ds(pl.multiple_of(y * HALF + q * 256, 256), 256)
            here = slice(q * 256, q * 256 + 256)
            dep_own = dep_ref[:, here]
            dep_other = dep_in[:, here].astype(jnp.float32)
            fade_own = infl_ref[SPAN - 8 : SPAN, lanes][7:8]
            fade_other = fade_in[7:8, here]
            dep_0 = jnp.where(is_first, dep_own, dep_other)
            dep_1 = jnp.where(is_first, dep_other, dep_own)
            fade_0 = jnp.where(is_first, fade_own, fade_other)
            fade_1 = jnp.where(is_first, fade_other, fade_own)
            slab = fade_1 * dep_0 + dep_1
            slab_fade = fade_0 * fade_1

            @pl.when(z > 0)
            def _():
                chain_copies[q].wait_recv()

            entering_0 = chain_in[q].astype(jnp.float32)
            chain_out[q] = (slab_fade * entering_0 + slab).astype(jnp.bfloat16)

            @pl.when(z < 3)
            def _():
                chain_copies[q].start()

            entering_1 = fade_0 * entering_0 + dep_0
            state_own[:, here] = jnp.where(is_first, entering_0, entering_1).astype(jnp.bfloat16)
            state_out[q] = jnp.where(is_first, entering_1, entering_0).astype(jnp.bfloat16)
            state_copies[q].start()

    @pl.loop(0, 3)
    def _(phase):
        late = jnp.where(z >= 2, 1, 0)

        @pl.when(phase != 1 + late)
        def _():
            mixing_of(jnp.where(phase == 0, 1 - y, y))

        @pl.when(phase == 1 + late)
        def _():
            chain()

    @pl.when(z == 0)
    def _():
        weight_copies[1].start()
        weight_copies[2].start()

    @pl.when(z % 2 == 0)
    def _():
        for copy in weight_copies[3:]:
            copy.start()

    gate_copy.wait()

    def act_copy(slot, half, quarter):
        source = 2 if slot == 3 else 0
        rows = pl.ds(quarter * 128, 128)
        return remote(
            acts.at[source, half, rows],
            acts.at[slot, half, rows],
            act_send.at[slot - 1, half, quarter],
            act_recv.at[slot - 1, half, quarter],
            z_pair if slot == 2 else y_pair,
        )

    def norm_half(half, state):
        lanes = pl.ds(pl.multiple_of(half * HALF, HALF), HALF)
        reads_at = pl.ds(pl.multiple_of(256 + half * 128, 128), 128)
        for quarter in range(2):

            @pl.loop(0, 2)
            def _(i):
                rows = pl.ds(pl.multiple_of(quarter * 128 + i * 64, 64), 64)
                read = jnp.dot(sconv[rows, reads_at], state, preferred_element_type=jnp.float32)
                gate = gate_ref[rows, lanes].astype(jnp.float32)
                scan = part_ref[rows, lanes] + infl_ref[rows, lanes] * read
                gated = scan * (gate * jax.nn.sigmoid(gate))
                mean = jnp.sum(gated * gated, axis=1, keepdims=True) * (1.0 / HALF)
                normed = gated * lax.rsqrt(mean + 1e-05) * gain_ref[:, lanes]
                acts[0, half, rows, :] = normed.astype(jnp.bfloat16)

            act_copy(2, half, quarter).start()
            act_copy(1, half, quarter).start()

    norm_half(y, state_own[...])
    for q in range(4):
        state_copies[q].wait_recv()
    norm_half(1 - y, jnp.concatenate([state_in[q] for q in range(4)], axis=1))

    def sum_copy(k, side, o):
        to = h ^ o
        rows = pl.ds(pl.multiple_of(to * 64, 64), 64)
        return remote(
            partial.at[k, side, rows],
            sums_in.at[k, side, o - 1],
            sum_send.at[k, side, o - 1],
            sum_recv.at[k, side, o - 1],
            s,
            to,
        )

    def project(k, side):
        weight = (weight_ref, weight_in)[side]

        @pl.loop(0, 2)
        def _(i):
            lanes = pl.ds(pl.multiple_of(i * 256, 256), 256)
            total = jnp.dot(
                acts[k, 0], weight[0:HALF, lanes], preferred_element_type=jnp.float32
            ) + jnp.dot(
                acts[k, 1], weight[HALF:CHANNELS, lanes], preferred_element_type=jnp.float32
            )
            partial_own[k, side, :, lanes] = total
            partial[k, side, :, lanes] = total.astype(jnp.bfloat16)

        for o in (2, 3, 1):
            sum_copy(k, side, o).start()

    rows_own = pl.ds(pl.multiple_of(h * 64, 64), 64)
    spot_own = pl.ds(pl.multiple_of(y * 512, 512), 512)

    def final_part(k, side):
        zt = z if k < 2 else z_far
        head = z if side == 0 else z_near
        copy = remote(
            final_out.at[k, side],
            final_in.at[rows_own, spot_own],
            final_send.at[k, side],
            final_recv.at[y * 4 + h],
            2 * zt + (y if k % 2 == 0 else 1 - y),
            head,
        )
        return copy, (head == h if k == 0 else None)

    def finish(k, side):
        for o in (1, 2, 3):
            sum_copy(k, side, o).wait_recv()
        total = partial_own[k, side, rows_own, :]
        for o in range(3):
            total = total + sums_in[k, side, o].astype(jnp.float32)
        final_out[k, side] = total.astype(jnp.bfloat16)
        copy, stays = final_part(k, side)
        if stays is None:
            copy.start()
            return

        @pl.when(stays)
        def _():
            final_in[rows_own, spot_own] = final_out[k, side]

        @pl.when(jnp.logical_not(stays))
        def _():
            copy.start()

    def arrived(slot, half):
        for quarter in range(2):
            act_copy(slot, half, quarter).wait_recv()
            if slot == 2:
                act_copy(3, half, quarter).start()

    weight_copy.wait()
    project(0, 0)
    arrived(1, 1 - y)
    arrived(1, y)
    project(1, 0)
    finish(0, 0)
    arrived(2, y)
    for copy in weight_copies:
        copy.wait_recv()
    project(0, 1)
    finish(1, 0)
    project(1, 1)
    finish(0, 1)
    arrived(2, 1 - y)
    project(2, 0)
    finish(1, 1)
    project(2, 1)
    finish(2, 0)
    arrived(3, 1 - y)
    arrived(3, y)
    project(3, 0)
    finish(2, 1)
    project(3, 1)
    finish(3, 0)
    finish(3, 1)

    z_from = 2 * (h // 2) + z % 2
    for y_from in range(2):
        for h_from in range(4):
            rows = slice(h_from * 64, h_from * 64 + 64)
            spot = slice(y_from * 512, y_from * 512 + 512)
            mine = (z_from == z) & (y_from == y) & (h_from == h)

            @pl.when(jnp.logical_not(mine))
            def _():
                remote(
                    final_out.at[0, 0],
                    final_in.at[rows, spot],
                    final_send.at[0, 0],
                    final_recv.at[y_from * 4 + h_from],
                    2 * z_from + y_from,
                    h_from,
                ).wait_recv()

    out_ref[...] = final_in[...]

    @pl.when(s < 7)
    def _():
        for copy in halo_copies:
            copy.wait_send()

    send_dep.wait_send()
    send_fade.wait_send()
    for copy in weight_copies:
        copy.wait_send()
    for q in range(4):
        state_copies[q].wait_send()

        @pl.when(z < 3)
        def _():
            chain_copies[q].wait_send()

    for slot in (1, 2, 3):
        for half in range(2):
            for quarter in range(2):
                act_copy(slot, half, quarter).wait_send()
    for k in range(4):
        for side in range(2):
            for o in (1, 2, 3):
                sum_copy(k, side, o).wait_send()
            copy, stays = final_part(k, side)
            if stays is None:
                copy.wait_send()
            else:

                @pl.when(jnp.logical_not(stays))
                def _():
                    copy.wait_send()


def on_device_fast(
    inner_input,
    state_input,
    gate_input,
    step_input,
    decay_exponent,
    skip_gain,
    documents,
    filter_inner,
    filter_state,
    norm_gain,
    output_weight,
):
    vmem = pl.BlockSpec(memory_space=pltpu.VMEM)
    smem = pl.BlockSpec(memory_space=pltpu.SMEM)
    anywhere = pl.BlockSpec(memory_space=pl.ANY)
    bf16, f32 = jnp.bfloat16, jnp.float32
    dma = pltpu.SemaphoreType.DMA
    return pl.pallas_call(
        fused_kernel,
        out_shape=jax.ShapeDtypeStruct((SPAN, 1024), bf16),
        in_specs=[vmem] * 8 + [smem] + [anywhere] * 2,
        out_specs=vmem,
        scratch_shapes=[
            pltpu.VMEM((SPAN, CHANNELS), bf16),
            pltpu.VMEM((CHANNELS, 512), bf16),
            pltpu.VMEM((CHANNELS, 512), bf16),
            pltpu.VMEM((16, CHANNELS), bf16),
            pltpu.VMEM((16, 512), bf16),
            pltpu.VMEM((1, SPAN), jnp.int32),
            pltpu.VMEM((SPAN + 16, 256), f32),
            pltpu.VMEM((SPAN, CHANNELS), bf16),
            pltpu.VMEM((SPAN, 512), bf16),
            pltpu.VMEM((32, SPAN), f32),
            pltpu.VMEM((32, SPAN), f32),
            pltpu.VMEM((32, SPAN), f32),
            pltpu.VMEM((32, SPAN), f32),
            pltpu.VMEM((SPAN, HALF), bf16),
            pltpu.VMEM((SPAN, CHANNELS), f32),
            pltpu.VMEM((SPAN, CHANNELS), f32),
            pltpu.VMEM((STATE, HALF), f32),
            pltpu.VMEM((STATE, HALF), bf16),
            pltpu.VMEM((STATE, HALF), bf16),
            pltpu.VMEM((8, HALF), f32),
            pltpu.VMEM((8, HALF), f32),
            pltpu.VMEM((4, STATE, 256), bf16),
            pltpu.VMEM((4, STATE, 256), bf16),
            pltpu.VMEM((4, STATE, 256), bf16),
            pltpu.VMEM((4, STATE, 256), bf16),
            pltpu.VMEM((STATE, HALF), bf16),
            pltpu.VMEM((4, 2, SPAN, HALF), bf16),
            pltpu.VMEM((4, 2, SPAN, 512), bf16),
            pltpu.VMEM((4, 2, SPAN, 512), f32),
            pltpu.VMEM((4, 2, 3, 64, 512), bf16),
            pltpu.VMEM((4, 2, 64, 512), bf16),
            pltpu.VMEM((SPAN, 1024), bf16),
            dma((2,)),
            dma((2, 3)),
            dma((2, 8)),
            dma((4,)),
            dma((2, 4)),
            dma((2, 4)),
            dma((3, 2, 2)),
            dma((3, 2, 2)),
            dma((4, 2, 3)),
            dma((4, 2, 3)),
            dma((4, 2)),
            dma((8,)),
        ],
        compiler_params=pltpu.CompilerParams(
            vmem_limit_bytes=56 * MIB, collective_id=0, has_side_effects=True
        ),
        name="layer",
    )(
        inner_input,
        state_input.reshape(SPAN, 512),
        step_input,
        decay_exponent[None, :],
        documents[None, :],
        filter_inner,
        filter_state.reshape(KERNEL, 512),
        norm_gain[None, :],
        skip_gain,
        gate_input,
        output_weight,
    )


def solution(mesh):
    placed = (
        P("seq", "head"),
        P("seq", None, "head"),
        P("seq", "head"),
        P("head", "seq"),
        P("head"),
        P("head"),
        P("seq"),
        P(None, "head"),
        P(None, None, "head"),
        P("head"),
        P("head", "seq"),
    )
    ways = dict(mesh.shape)
    fast = ways["seq"] == 8 and ways["head"] == 4
    return jax.shard_map(
        on_device_fast if fast else on_device, mesh=mesh, in_specs=placed, out_specs=P("seq", "head"), check_vma=False
    )
```

```python
import jax
import jax.numpy as jnp
from jax import lax
from jax.experimental import pallas as pl
from jax.experimental.pallas import tpu as pltpu
from jax.sharding import PartitionSpec as P

HEAD_DIM = 64
STATE = 128
GROUPS = 8
INNER = 8192
KERNEL = 4


highest = lax.Precision.HIGHEST


def entering(part, axis, combine, identity):
    place = lax.axis_index(axis)
    gathered = jax.tree.map(lambda a: lax.all_gather(a, axis), part)
    state = jax.tree.map(lambda a, e: jnp.zeros_like(a) + jnp.asarray(e, a.dtype), part, identity)

    def one(step, state):
        return combine(
            state, jax.tree.map(lambda a: lax.dynamic_index_in_dim(a, step, 0, False), gathered)
        )

    return lax.fori_loop(0, place, one, state)


def passed_along(value, axis, steps):
    count = lax.axis_size(axis)
    initial, last = (max(0, -steps), min(count, count - steps))
    return lax.ppermute(value, axis, [(source, source + steps) for source in range(initial, last)])


def causal_conv(extended, weights, segments_wide, segment_block):
    length = segment_block.shape[0]
    running = jnp.zeros(extended[:length].shape, jnp.float32)
    for offset in range(KERNEL):
        window = extended[offset : offset + length].astype(jnp.float32)
        matches = segments_wide[offset : offset + length] == segment_block
        matches = matches.reshape((length,) + (1,) * (extended.ndim - 1))
        running = running + jnp.where(matches, window * weights[offset], jnp.float32(0.0))
    return jax.nn.silu(running).astype(jnp.bfloat16)


def span_parts(values, write_rows, read_rows, step_size, decay_rate, segment_block, prior_segment):
    length = segment_block.shape[0]
    repeat = decay_rate.shape[0] // write_rows.shape[1]
    cumulative = jnp.cumsum(decay_rate, axis=1)
    places = jnp.arange(length)
    linked = (segment_block[:, None] == segment_block[None, :]) & (
        places[:, None] >= places[None, :]
    )
    spread = cumulative[:, :, None] - cumulative[:, None, :]
    decays = jnp.exp(jnp.where(linked[None], spread, -jnp.inf))
    scores = jnp.einsum("ign,jgn->gij", read_rows, write_rows, preferred_element_type=jnp.float32)
    scores = jnp.repeat(scores, repeat, axis=0)
    mixing = (decays * scores * step_size[:, None, :]).astype(jnp.bfloat16)
    within = jnp.einsum("hij,jhp->ihp", mixing, values, preferred_element_type=jnp.float32)
    inflow = jnp.exp(cumulative) * (segment_block == prior_segment)[None, :].astype(jnp.float32)
    final_segment = segment_block[-1]
    closing = (
        jnp.exp(cumulative[:, -1:] - cumulative)
        * (segment_block == final_segment)[None, :].astype(jnp.float32)
        * step_size
    )
    weighted = (values.astype(jnp.float32) * closing.T[:, :, None]).astype(jnp.bfloat16)
    writes = jnp.repeat(write_rows, repeat, axis=1)
    deposit = jnp.einsum("jhp,jhn->hpn", weighted, writes, preferred_element_type=jnp.float32)
    fading = jnp.exp(cumulative[:, -1]) * (final_segment == prior_segment).astype(jnp.float32)
    return (within, inflow, fading, deposit)


def reading(read_rows, held_state, repeat):
    readers = jnp.repeat(read_rows, repeat, axis=1).astype(jnp.float32)
    return jnp.einsum("ihn,hpn->ihp", readers, held_state, precision=highest)


def gated_norm(outputs, gates, norm_scale):
    height = outputs.shape[0]
    gated = outputs * jax.nn.silu(gates.astype(jnp.float32))
    grouped = gated.reshape(height, -1, INNER // GROUPS)
    mean_square = jnp.mean(grouped * grouped, axis=-1, keepdims=True)
    normed = (grouped * lax.rsqrt(mean_square + 1e-05)).reshape(height, -1) * norm_scale
    return normed.astype(jnp.bfloat16)


def chain_states(through, local_state):

    def combine_pair(earlier, later):
        return (earlier[0] * later[0], later[0][:, None, None] * earlier[1] + later[1])

    neutral = (jnp.ones_like(through), jnp.zeros_like(local_state))
    return entering((through, local_state), "seq", combine_pair, neutral)[1]


def on_device(
    inner_input,
    state_input,
    gate_input,
    step_input,
    decay_exponent,
    skip_gain,
    documents,
    filter_inner,
    filter_state,
    norm_gain,
    output_weight,
):
    margin = KERNEL - 1
    length = documents.shape[0]
    head_count = decay_exponent.shape[0]
    groups = state_input.shape[2] // STATE
    repeat = head_count // groups
    before_inner, before_state, before_segments = passed_along(
        (inner_input[-margin:], state_input[-margin:], documents[-margin:].astype(jnp.bfloat16)),
        "seq",
        1,
    )
    segments_wide = jnp.concatenate([before_segments.astype(jnp.int32), documents])
    inner_conv = causal_conv(
        jnp.concatenate([before_inner, inner_input]), filter_inner, segments_wide, documents
    )
    state_conv = causal_conv(
        jnp.concatenate([before_state, state_input]), filter_state, segments_wide, documents
    )
    values = inner_conv.reshape(length, head_count, HEAD_DIM)
    write_rows = state_conv[:, 0].reshape(length, groups, STATE)
    read_rows = state_conv[:, 1].reshape(length, groups, STATE)
    step_size = jax.nn.softplus(step_input)
    decay_rate = -step_size * jnp.exp(decay_exponent)[:, None]
    skipped = skip_gain[None, :, None] * values.astype(jnp.float32)
    prior_segment = segments_wide[margin - 1]
    pieces = [
        span_parts(values, write_rows, read_rows, step_size, decay_rate, documents, prior_segment)
    ]
    local_state = jnp.zeros((head_count, HEAD_DIM, STATE), jnp.float32)
    through = jnp.ones((head_count,), jnp.float32)
    block_index = 0
    within, inflow, fading, deposit = pieces[block_index]
    local_state = fading[:, None, None] * local_state + deposit
    through = through * fading
    carried = chain_states(through, local_state)
    block_index = 0
    within, inflow, fading, deposit = pieces[block_index]
    outputs = within + inflow.T[:, :, None] * reading(read_rows, carried, repeat) + skipped
    scan_out = outputs.reshape(length, head_count * HEAD_DIM)
    normed = gated_norm(scan_out, gate_input, norm_gain)
    partial_value = jnp.dot(
        normed,
        lax.all_gather(output_weight, "seq", axis=1, tiled=True),
        preferred_element_type=jnp.float32,
    )
    return lax.psum_scatter(partial_value, "head", scatter_dimension=1, tiled=True).astype(
        jnp.bfloat16
    )


MESH = pl.DeviceIdType.MESH
SPAN = 256
CHANNELS = 2048
HALF = 1024
MIB = 1 << 20


def fused_kernel(
    inner_ref,
    state_ref,
    step_ref,
    decay_ref,
    documents_ref,
    filter_inner_ref,
    filter_state_ref,
    gain_ref,
    skip_ref,
    gate_hbm,
    weight_hbm,
    out_ref,
    gate_ref,
    weight_ref,
    weight_in,
    halo_inner,
    halo_state,
    halo_documents,
    ext,
    conv,
    sconv,
    cum_rows,
    step_rows,
    in_rows,
    close_rows,
    weighted,
    part_ref,
    infl_ref,
    dep_ref,
    dep_stage,
    dep_in,
    fade_stage,
    fade_in,
    chain_out,
    chain_in,
    state_out,
    state_in,
    state_own,
    acts,
    partial,
    partial_own,
    sums_in,
    final_out,
    final_in,
    local_sems,
    halo_sems,
    weight_sems,
    pair_sems,
    chain_sems,
    state_sems,
    act_send,
    act_recv,
    sum_send,
    sum_recv,
    final_send,
    final_recv,
):
    s = lax.axis_index("seq")
    h = lax.axis_index("head")
    z, y = s // 2, s % 2
    me = s * 4 + h
    z_near = z + 1 - 2 * (z % 2)
    z_far = (z + 2) % 4
    y_pair = 2 * z + 1 - y
    z_pair = 2 * z_far + y

    def remote(src, dst, send, recv, seq, head=h):
        return pltpu.make_async_remote_copy(
            src_ref=src,
            dst_ref=dst,
            send_sem=send,
            recv_sem=recv,
            device_id=(seq, head),
            device_id_type=MESH,
        )

    gate_copy = pltpu.make_async_copy(gate_hbm, gate_ref, local_sems.at[0])
    weight_copy = pltpu.make_async_copy(weight_hbm, weight_ref, local_sems.at[1])
    gate_copy.start()
    weight_copy.start()

    barrier = pltpu.get_barrier_semaphore()

    @pl.loop(1, 32)
    def _(i):
        other = lax.rem(me + i, 32)
        pl.semaphore_signal(
            barrier, inc=1, device_id=(other // 4, other % 4), device_id_type=MESH
        )

    pl.semaphore_wait(barrier, 31)

    after = jnp.minimum(s + 1, 7)
    halo_copies = [
        remote(source, target, halo_sems.at[0, i], halo_sems.at[1, i], after)
        for i, (source, target) in enumerate(
            (
                (documents_ref, halo_documents),
                (state_ref.at[pl.ds(SPAN - 16, 16)], halo_state),
                (inner_ref.at[pl.ds(SPAN - 16, 16)], halo_inner),
            )
        )
    ]

    @pl.when(s < 7)
    def _():
        for copy in halo_copies:
            copy.start()

    weight_copies = []
    for i in range(8):
        rows = pl.ds(i * 256, 256)
        weight_copies.append(
            remote(
                weight_hbm.at[rows],
                weight_in.at[rows],
                weight_sems.at[0, i],
                weight_sems.at[1, i],
                2 * z_near + y,
            )
        )
    weight_copies[0].start()

    @pl.when(z > 0)
    def _():
        weight_copies[1].start()
        weight_copies[2].start()

    @pl.when(z % 2 == 1)
    def _():
        for copy in weight_copies[3:]:
            copy.start()

    @pl.when(s == 0)
    def _():
        halo_documents[...] = jnp.zeros_like(halo_documents)
        halo_state[...] = jnp.zeros_like(halo_state)
        halo_inner[...] = jnp.zeros_like(halo_inner)

    diagonal = lax.broadcasted_iota(jnp.int32, (32, 32), 0) == lax.broadcasted_iota(
        jnp.int32, (32, 32), 1
    )
    rate = jnp.sum(
        jnp.where(diagonal, jnp.broadcast_to(jnp.exp(decay_ref[...]), (32, 32)), 0.0),
        axis=1,
        keepdims=True,
    )
    value = step_ref[...]
    step = jnp.maximum(value, 0.0) + jnp.log1p(jnp.exp(-jnp.abs(value)))
    row_at = lax.broadcasted_iota(jnp.int32, (SPAN, SPAN), 0)
    col_at = lax.broadcasted_iota(jnp.int32, (SPAN, SPAN), 1)
    upper = (row_at <= col_at).astype(jnp.float32)
    cumulative = jnp.dot(
        -step * rate, upper, precision=highest, preferred_element_type=jnp.float32
    )
    documents = documents_ref[...].astype(jnp.float32)
    final = (documents == documents[:, SPAN - 1 :]).astype(jnp.float32)
    step_rows[...] = step
    cum_rows[...] = cumulative
    close_rows[...] = jnp.exp(cumulative[:, SPAN - 1 :] - cumulative) * final * step

    @pl.when(s > 0)
    def _():
        for copy in halo_copies:
            copy.wait_recv()

    before = halo_documents[...].astype(jnp.float32)
    in_rows[...] = jnp.exp(cumulative) * (documents == before[:, SPAN - 1 :]).astype(jnp.float32)
    lane = lax.broadcasted_iota(jnp.int32, (8, SPAN), 1)
    mark_row = lax.broadcasted_iota(jnp.int32, (8, SPAN), 0)
    documents_8 = jnp.broadcast_to(documents, (8, SPAN))
    before_8 = jnp.broadcast_to(before, (8, SPAN))
    mark_rows = documents_8
    for k in (1, 2, 3):
        shifted = jnp.where(
            lane < k, pltpu.roll(before_8, k, axis=1), pltpu.roll(documents_8, k, axis=1)
        )
        same = (shifted == documents_8).astype(jnp.float32)
        mark_rows = jnp.where(mark_row == k, same, mark_rows)
    marks = mark_rows.T

    def convolve(source, halo, at, taps, target):
        lanes = pl.ds(at, 256)
        ext[0:16, :] = halo[:, lanes].astype(jnp.float32)
        ext[16:272, :] = source[:, lanes].astype(jnp.float32)
        running = marks[:, 3:4] * (ext[13:269, :] * taps(0, lanes))
        running = running + marks[:, 2:3] * (ext[14:270, :] * taps(1, lanes))
        running = running + marks[:, 1:2] * (ext[15:271, :] * taps(2, lanes))
        running = running + ext[16:272, :] * taps(3, lanes)
        target[:, lanes] = (running * jax.nn.sigmoid(running)).astype(jnp.bfloat16)

    for i in range(2):
        convolve(
            state_ref,
            halo_state,
            i * 256,
            lambda k, lanes, i=i: filter_state_ref[k, i : i + 1, :],
            sconv,
        )

    linked = (marks[:, 0:1] == documents) & (row_at >= col_at)
    low = lax.broadcasted_iota(jnp.int32, (SPAN, 128), 1) < HEAD_DIM

    apart = pl.ds(pl.multiple_of((1 - y) * HALF, HALF), HALF)
    send_dep = remote(dep_stage, dep_in, pair_sems.at[0], pair_sems.at[1], y_pair)
    send_fade = remote(fade_stage, fade_in, pair_sems.at[2], pair_sems.at[3], y_pair)

    @pl.loop(0, 2)
    def _(turn):
        group = jnp.where(turn == 0, 1 - y, y)
        base = group * HALF

        @pl.loop(0, 4)
        def _(i):
            at = pl.multiple_of(base + i * 256, 256)
            convolve(
                inner_ref,
                halo_inner,
                at,
                lambda k, lanes: filter_inner_ref[k : k + 1, lanes],
                conv,
            )

        writes = sconv[:, pl.ds(pl.multiple_of(group * 128, 128), 128)]
        heads = pl.ds(pl.multiple_of(group * 16, 16), 16)
        in_cols = in_rows[heads, :].T
        close_cols = close_rows[heads, :].T
        for pair in range(8):
            first = pair * 2
            at = pl.ds(pl.multiple_of(base + pair * 128, 128), 128)

            def both(cols):
                return jnp.where(low, cols[:, first : first + 1], cols[:, first + 1 : first + 2])

            weighted[:, pair * 128 : pair * 128 + 128] = (
                conv[:, at].astype(jnp.float32) * both(close_cols)
            ).astype(jnp.bfloat16)
            infl_ref[:, at] = both(in_cols)
        dep_ref[...] = lax.dot_general(
            writes, weighted[...], (((0,), (0,)), ((), ())), preferred_element_type=jnp.float32
        )

        @pl.when(turn == 0)
        def _():
            dep_stage[...] = dep_ref[...].astype(jnp.bfloat16)
            fade_stage[...] = infl_ref[SPAN - 8 : SPAN, apart]
            send_fade.start()
            send_dep.start()

    def mixing_of(group):
        base = group * HALF
        writes = sconv[:, pl.ds(pl.multiple_of(group * 128, 128), 128)]
        reads = sconv[:, pl.ds(pl.multiple_of(256 + group * 128, 128), 128)]
        scores = lax.dot_general(
            reads, writes, (((1,), (1,)), ((), ())), preferred_element_type=jnp.float32
        )
        scores = jnp.where(linked, scores, 0.0)
        heads = pl.ds(pl.multiple_of(group * 16, 16), 16)
        cums = cum_rows[heads, :]
        steps = step_rows[heads, :]
        cum_cols = cums.T
        for pair in range(8):
            first = pair * 2
            at = pl.ds(pl.multiple_of(base + pair * 128, 128), 128)
            x = conv[:, at]

            def mixed(j):
                spread = jnp.minimum(cum_cols[:, j : j + 1] - cums[j : j + 1, :], 0.0)
                mixing = (jnp.exp(spread) * scores * steps[j : j + 1, :]).astype(jnp.bfloat16)
                return jnp.dot(mixing, x, preferred_element_type=jnp.float32)

            gain = jnp.where(low, skip_ref[group * 16 + first], skip_ref[group * 16 + first + 1])
            part_ref[:, at] = jnp.where(low, mixed(first), mixed(first + 1)) + gain * x.astype(
                jnp.float32
            )

    @pl.when(z == 0)
    def _():
        chain_in[...] = jnp.zeros_like(chain_in)

    is_first = y == 0
    chain_copies = [
        remote(
            chain_out.at[q],
            chain_in.at[q],
            chain_sems.at[0, q],
            chain_sems.at[1, q],
            jnp.minimum(s + 2, 7),
        )
        for q in range(4)
    ]
    state_copies = [
        remote(state_out.at[q], state_in.at[q], state_sems.at[0, q], state_sems.at[1, q], y_pair)
        for q in range(4)
    ]
    def chain():
        send_fade.wait_recv()
        send_dep.wait_recv()
        for q in range(4):
            lanes = pl.ds(pl.multiple_of(y * HALF + q * 256, 256), 256)
            here = slice(q * 256, q * 256 + 256)
            dep_own = dep_ref[:, here]
            dep_other = dep_in[:, here].astype(jnp.float32)
            fade_own = infl_ref[SPAN - 8 : SPAN, lanes][7:8]
            fade_other = fade_in[7:8, here]
            dep_0 = jnp.where(is_first, dep_own, dep_other)
            dep_1 = jnp.where(is_first, dep_other, dep_own)
            fade_0 = jnp.where(is_first, fade_own, fade_other)
            fade_1 = jnp.where(is_first, fade_other, fade_own)
            slab = fade_1 * dep_0 + dep_1
            slab_fade = fade_0 * fade_1

            @pl.when(z > 0)
            def _():
                chain_copies[q].wait_recv()

            entering_0 = chain_in[q].astype(jnp.float32)
            chain_out[q] = (slab_fade * entering_0 + slab).astype(jnp.bfloat16)

            @pl.when(z < 3)
            def _():
                chain_copies[q].start()

            entering_1 = fade_0 * entering_0 + dep_0
            state_own[:, here] = jnp.where(is_first, entering_0, entering_1).astype(jnp.bfloat16)
            state_out[q] = jnp.where(is_first, entering_1, entering_0).astype(jnp.bfloat16)
            state_copies[q].start()

    @pl.loop(0, 3)
    def _(phase):
        late = jnp.where(z >= 2, 1, 0)

        @pl.when(phase != 1 + late)
        def _():
            mixing_of(jnp.where(phase == 0, 1 - y, y))

        @pl.when(phase == 1 + late)
        def _():
            chain()

    @pl.when(z == 0)
    def _():
        weight_copies[1].start()
        weight_copies[2].start()

    @pl.when(z % 2 == 0)
    def _():
        for copy in weight_copies[3:]:
            copy.start()

    gate_copy.wait()

    def act_copy(slot, half, quarter):
        source = 2 if slot == 3 else 0
        rows = pl.ds(quarter * 128, 128)
        return remote(
            acts.at[source, half, rows],
            acts.at[slot, half, rows],
            act_send.at[slot - 1, half, quarter],
            act_recv.at[slot - 1, half, quarter],
            z_pair if slot == 2 else y_pair,
        )

    def norm_half(half, state):
        lanes = pl.ds(pl.multiple_of(half * HALF, HALF), HALF)
        reads_at = pl.ds(pl.multiple_of(256 + half * 128, 128), 128)
        for quarter in range(2):

            @pl.loop(0, 2)
            def _(i):
                rows = pl.ds(pl.multiple_of(quarter * 128 + i * 64, 64), 64)
                read = jnp.dot(sconv[rows, reads_at], state, preferred_element_type=jnp.float32)
                gate = gate_ref[rows, lanes].astype(jnp.float32)
                scan = part_ref[rows, lanes] + infl_ref[rows, lanes] * read
                gated = scan * (gate * jax.nn.sigmoid(gate))
                mean = jnp.sum(gated * gated, axis=1, keepdims=True) * (1.0 / HALF)
                normed = gated * lax.rsqrt(mean + 1e-05) * gain_ref[:, lanes]
                acts[0, half, rows, :] = normed.astype(jnp.bfloat16)

            act_copy(2, half, quarter).start()
            act_copy(1, half, quarter).start()

    norm_half(y, state_own[...])
    for q in range(4):
        state_copies[q].wait_recv()
    norm_half(1 - y, jnp.concatenate([state_in[q] for q in range(4)], axis=1))

    def sum_copy(k, side, o):
        to = h ^ o
        rows = pl.ds(pl.multiple_of(to * 64, 64), 64)
        return remote(
            partial.at[k, side, rows],
            sums_in.at[k, side, o - 1],
            sum_send.at[k, side, o - 1],
            sum_recv.at[k, side, o - 1],
            s,
            to,
        )

    def project(k, side):
        weight = (weight_ref, weight_in)[side]

        @pl.loop(0, 2)
        def _(i):
            lanes = pl.ds(pl.multiple_of(i * 256, 256), 256)
            total = jnp.dot(
                acts[k, 0], weight[0:HALF, lanes], preferred_element_type=jnp.float32
            ) + jnp.dot(
                acts[k, 1], weight[HALF:CHANNELS, lanes], preferred_element_type=jnp.float32
            )
            partial_own[k, side, :, lanes] = total
            partial[k, side, :, lanes] = total.astype(jnp.bfloat16)

        for o in (2, 3, 1):
            sum_copy(k, side, o).start()

    rows_own = pl.ds(pl.multiple_of(h * 64, 64), 64)
    spot_own = pl.ds(pl.multiple_of(y * 512, 512), 512)

    def final_part(k, side):
        zt = z if k < 2 else z_far
        head = z if side == 0 else z_near
        copy = remote(
            final_out.at[k, side],
            final_in.at[rows_own, spot_own],
            final_send.at[k, side],
            final_recv.at[y * 4 + h],
            2 * zt + (y if k % 2 == 0 else 1 - y),
            head,
        )
        return copy, (head == h if k == 0 else None)

    def finish(k, side):
        for o in (1, 2, 3):
            sum_copy(k, side, o).wait_recv()
        total = partial_own[k, side, rows_own, :]
        for o in range(3):
            total = total + sums_in[k, side, o].astype(jnp.float32)
        final_out[k, side] = total.astype(jnp.bfloat16)
        copy, stays = final_part(k, side)
        if stays is None:
            copy.start()
            return

        @pl.when(stays)
        def _():
            final_in[rows_own, spot_own] = final_out[k, side]

        @pl.when(jnp.logical_not(stays))
        def _():
            copy.start()

    def arrived(slot, half):
        for quarter in range(2):
            act_copy(slot, half, quarter).wait_recv()
            if slot == 2:
                act_copy(3, half, quarter).start()

    weight_copy.wait()
    project(0, 0)
    arrived(1, 1 - y)
    arrived(1, y)
    project(1, 0)
    finish(0, 0)
    arrived(2, y)
    finish(1, 0)

    def first_blocks():
        for copy in weight_copies:
            copy.wait_recv()
        project(0, 1)
        project(1, 1)
        finish(0, 1)

    @pl.when(z < 3)
    def _():
        first_blocks()

    arrived(2, 1 - y)
    project(2, 0)

    @pl.when(z < 3)
    def _():
        finish(1, 1)

    finish(2, 0)

    @pl.when(z == 3)
    def _():
        first_blocks()
        finish(1, 1)

    project(2, 1)
    arrived(3, 1 - y)
    arrived(3, y)
    project(3, 0)
    finish(2, 1)
    project(3, 1)
    finish(3, 0)
    finish(3, 1)

    z_from = 2 * (h // 2) + z % 2
    for y_from in range(2):
        for h_from in range(4):
            rows = slice(h_from * 64, h_from * 64 + 64)
            spot = slice(y_from * 512, y_from * 512 + 512)
            mine = (z_from == z) & (y_from == y) & (h_from == h)

            @pl.when(jnp.logical_not(mine))
            def _():
                remote(
                    final_out.at[0, 0],
                    final_in.at[rows, spot],
                    final_send.at[0, 0],
                    final_recv.at[y_from * 4 + h_from],
                    2 * z_from + y_from,
                    h_from,
                ).wait_recv()

    out_ref[...] = final_in[...]

    @pl.when(s < 7)
    def _():
        for copy in halo_copies:
            copy.wait_send()

    send_dep.wait_send()
    send_fade.wait_send()
    for copy in weight_copies:
        copy.wait_send()
    for q in range(4):
        state_copies[q].wait_send()

        @pl.when(z < 3)
        def _():
            chain_copies[q].wait_send()

    for slot in (1, 2, 3):
        for half in range(2):
            for quarter in range(2):
                act_copy(slot, half, quarter).wait_send()
    for k in range(4):
        for side in range(2):
            for o in (1, 2, 3):
                sum_copy(k, side, o).wait_send()
            copy, stays = final_part(k, side)
            if stays is None:
                copy.wait_send()
            else:

                @pl.when(jnp.logical_not(stays))
                def _():
                    copy.wait_send()


def on_device_fast(
    inner_input,
    state_input,
    gate_input,
    step_input,
    decay_exponent,
    skip_gain,
    documents,
    filter_inner,
    filter_state,
    norm_gain,
    output_weight,
):
    vmem = pl.BlockSpec(memory_space=pltpu.VMEM)
    smem = pl.BlockSpec(memory_space=pltpu.SMEM)
    anywhere = pl.BlockSpec(memory_space=pl.ANY)
    bf16, f32 = jnp.bfloat16, jnp.float32
    dma = pltpu.SemaphoreType.DMA
    return pl.pallas_call(
        fused_kernel,
        out_shape=jax.ShapeDtypeStruct((SPAN, 1024), bf16),
        in_specs=[vmem] * 8 + [smem] + [anywhere] * 2,
        out_specs=vmem,
        scratch_shapes=[
            pltpu.VMEM((SPAN, CHANNELS), bf16),
            pltpu.VMEM((CHANNELS, 512), bf16),
            pltpu.VMEM((CHANNELS, 512), bf16),
            pltpu.VMEM((16, CHANNELS), bf16),
            pltpu.VMEM((16, 512), bf16),
            pltpu.VMEM((1, SPAN), jnp.int32),
            pltpu.VMEM((SPAN + 16, 256), f32),
            pltpu.VMEM((SPAN, CHANNELS), bf16),
            pltpu.VMEM((SPAN, 512), bf16),
            pltpu.VMEM((32, SPAN), f32),
            pltpu.VMEM((32, SPAN), f32),
            pltpu.VMEM((32, SPAN), f32),
            pltpu.VMEM((32, SPAN), f32),
            pltpu.VMEM((SPAN, HALF), bf16),
            pltpu.VMEM((SPAN, CHANNELS), f32),
            pltpu.VMEM((SPAN, CHANNELS), f32),
            pltpu.VMEM((STATE, HALF), f32),
            pltpu.VMEM((STATE, HALF), bf16),
            pltpu.VMEM((STATE, HALF), bf16),
            pltpu.VMEM((8, HALF), f32),
            pltpu.VMEM((8, HALF), f32),
            pltpu.VMEM((4, STATE, 256), bf16),
            pltpu.VMEM((4, STATE, 256), bf16),
            pltpu.VMEM((4, STATE, 256), bf16),
            pltpu.VMEM((4, STATE, 256), bf16),
            pltpu.VMEM((STATE, HALF), bf16),
            pltpu.VMEM((4, 2, SPAN, HALF), bf16),
            pltpu.VMEM((4, 2, SPAN, 512), bf16),
            pltpu.VMEM((4, 2, SPAN, 512), f32),
            pltpu.VMEM((4, 2, 3, 64, 512), bf16),
            pltpu.VMEM((4, 2, 64, 512), bf16),
            pltpu.VMEM((SPAN, 1024), bf16),
            dma((2,)),
            dma((2, 3)),
            dma((2, 8)),
            dma((4,)),
            dma((2, 4)),
            dma((2, 4)),
            dma((3, 2, 2)),
            dma((3, 2, 2)),
            dma((4, 2, 3)),
            dma((4, 2, 3)),
            dma((4, 2)),
            dma((8,)),
        ],
        compiler_params=pltpu.CompilerParams(
            vmem_limit_bytes=56 * MIB, collective_id=0, has_side_effects=True
        ),
        name="layer",
    )(
        inner_input,
        state_input.reshape(SPAN, 512),
        step_input,
        decay_exponent[None, :],
        documents[None, :],
        filter_inner,
        filter_state,
        norm_gain[None, :],
        skip_gain,
        gate_input,
        output_weight,
    )


def solution(mesh):
    placed = (
        P("seq", "head"),
        P("seq", None, "head"),
        P("seq", "head"),
        P("head", "seq"),
        P("head"),
        P("head"),
        P("seq"),
        P(None, "head"),
        P(None, None, "head"),
        P("head"),
        P("head", "seq"),
    )
    ways = dict(mesh.shape)
    fast = ways["seq"] == 8 and ways["head"] == 4
    return jax.shard_map(
        on_device_fast if fast else on_device, mesh=mesh, in_specs=placed, out_specs=P("seq", "head"), check_vma=False
    )
```

```python
import jax
import jax.numpy as jnp
from jax import lax
from jax.experimental import pallas as pl
from jax.experimental.pallas import tpu as pltpu
from jax.sharding import PartitionSpec as P

HEAD_DIM = 64
STATE = 128
GROUPS = 8
INNER = 8192
KERNEL = 4


highest = lax.Precision.HIGHEST


def entering(part, axis, combine, identity):
    place = lax.axis_index(axis)
    gathered = jax.tree.map(lambda a: lax.all_gather(a, axis), part)
    state = jax.tree.map(lambda a, e: jnp.zeros_like(a) + jnp.asarray(e, a.dtype), part, identity)

    def one(step, state):
        return combine(
            state, jax.tree.map(lambda a: lax.dynamic_index_in_dim(a, step, 0, False), gathered)
        )

    return lax.fori_loop(0, place, one, state)


def passed_along(value, axis, steps):
    count = lax.axis_size(axis)
    initial, last = (max(0, -steps), min(count, count - steps))
    return lax.ppermute(value, axis, [(source, source + steps) for source in range(initial, last)])


def causal_conv(extended, weights, segments_wide, segment_block):
    length = segment_block.shape[0]
    running = jnp.zeros(extended[:length].shape, jnp.float32)
    for offset in range(KERNEL):
        window = extended[offset : offset + length].astype(jnp.float32)
        matches = segments_wide[offset : offset + length] == segment_block
        matches = matches.reshape((length,) + (1,) * (extended.ndim - 1))
        running = running + jnp.where(matches, window * weights[offset], jnp.float32(0.0))
    return jax.nn.silu(running).astype(jnp.bfloat16)


def span_parts(values, write_rows, read_rows, step_size, decay_rate, segment_block, prior_segment):
    length = segment_block.shape[0]
    repeat = decay_rate.shape[0] // write_rows.shape[1]
    cumulative = jnp.cumsum(decay_rate, axis=1)
    places = jnp.arange(length)
    linked = (segment_block[:, None] == segment_block[None, :]) & (
        places[:, None] >= places[None, :]
    )
    spread = cumulative[:, :, None] - cumulative[:, None, :]
    decays = jnp.exp(jnp.where(linked[None], spread, -jnp.inf))
    scores = jnp.einsum("ign,jgn->gij", read_rows, write_rows, preferred_element_type=jnp.float32)
    scores = jnp.repeat(scores, repeat, axis=0)
    mixing = (decays * scores * step_size[:, None, :]).astype(jnp.bfloat16)
    within = jnp.einsum("hij,jhp->ihp", mixing, values, preferred_element_type=jnp.float32)
    inflow = jnp.exp(cumulative) * (segment_block == prior_segment)[None, :].astype(jnp.float32)
    final_segment = segment_block[-1]
    closing = (
        jnp.exp(cumulative[:, -1:] - cumulative)
        * (segment_block == final_segment)[None, :].astype(jnp.float32)
        * step_size
    )
    weighted = (values.astype(jnp.float32) * closing.T[:, :, None]).astype(jnp.bfloat16)
    writes = jnp.repeat(write_rows, repeat, axis=1)
    deposit = jnp.einsum("jhp,jhn->hpn", weighted, writes, preferred_element_type=jnp.float32)
    fading = jnp.exp(cumulative[:, -1]) * (final_segment == prior_segment).astype(jnp.float32)
    return (within, inflow, fading, deposit)


def reading(read_rows, held_state, repeat):
    readers = jnp.repeat(read_rows, repeat, axis=1).astype(jnp.float32)
    return jnp.einsum("ihn,hpn->ihp", readers, held_state, precision=highest)


def gated_norm(outputs, gates, norm_scale):
    height = outputs.shape[0]
    gated = outputs * jax.nn.silu(gates.astype(jnp.float32))
    grouped = gated.reshape(height, -1, INNER // GROUPS)
    mean_square = jnp.mean(grouped * grouped, axis=-1, keepdims=True)
    normed = (grouped * lax.rsqrt(mean_square + 1e-05)).reshape(height, -1) * norm_scale
    return normed.astype(jnp.bfloat16)


def chain_states(through, local_state):

    def combine_pair(earlier, later):
        return (earlier[0] * later[0], later[0][:, None, None] * earlier[1] + later[1])

    neutral = (jnp.ones_like(through), jnp.zeros_like(local_state))
    return entering((through, local_state), "seq", combine_pair, neutral)[1]


def on_device(
    inner_input,
    state_input,
    gate_input,
    step_input,
    decay_exponent,
    skip_gain,
    documents,
    filter_inner,
    filter_state,
    norm_gain,
    output_weight,
):
    margin = KERNEL - 1
    length = documents.shape[0]
    head_count = decay_exponent.shape[0]
    groups = state_input.shape[2] // STATE
    repeat = head_count // groups
    before_inner, before_state, before_segments = passed_along(
        (inner_input[-margin:], state_input[-margin:], documents[-margin:].astype(jnp.bfloat16)),
        "seq",
        1,
    )
    segments_wide = jnp.concatenate([before_segments.astype(jnp.int32), documents])
    inner_conv = causal_conv(
        jnp.concatenate([before_inner, inner_input]), filter_inner, segments_wide, documents
    )
    state_conv = causal_conv(
        jnp.concatenate([before_state, state_input]), filter_state, segments_wide, documents
    )
    values = inner_conv.reshape(length, head_count, HEAD_DIM)
    write_rows = state_conv[:, 0].reshape(length, groups, STATE)
    read_rows = state_conv[:, 1].reshape(length, groups, STATE)
    step_size = jax.nn.softplus(step_input)
    decay_rate = -step_size * jnp.exp(decay_exponent)[:, None]
    skipped = skip_gain[None, :, None] * values.astype(jnp.float32)
    prior_segment = segments_wide[margin - 1]
    pieces = [
        span_parts(values, write_rows, read_rows, step_size, decay_rate, documents, prior_segment)
    ]
    local_state = jnp.zeros((head_count, HEAD_DIM, STATE), jnp.float32)
    through = jnp.ones((head_count,), jnp.float32)
    block_index = 0
    within, inflow, fading, deposit = pieces[block_index]
    local_state = fading[:, None, None] * local_state + deposit
    through = through * fading
    carried = chain_states(through, local_state)
    block_index = 0
    within, inflow, fading, deposit = pieces[block_index]
    outputs = within + inflow.T[:, :, None] * reading(read_rows, carried, repeat) + skipped
    scan_out = outputs.reshape(length, head_count * HEAD_DIM)
    normed = gated_norm(scan_out, gate_input, norm_gain)
    partial_value = jnp.dot(
        normed,
        lax.all_gather(output_weight, "seq", axis=1, tiled=True),
        preferred_element_type=jnp.float32,
    )
    return lax.psum_scatter(partial_value, "head", scatter_dimension=1, tiled=True).astype(
        jnp.bfloat16
    )


MESH = pl.DeviceIdType.MESH
SPAN = 256
CHANNELS = 2048
HALF = 1024
MIB = 1 << 20


def fused_kernel(
    inner_ref,
    state_ref,
    step_ref,
    decay_ref,
    documents_ref,
    filter_inner_ref,
    filter_state_ref,
    gain_ref,
    skip_ref,
    gate_hbm,
    weight_hbm,
    out_ref,
    gate_ref,
    weight_ref,
    weight_in,
    halo_inner,
    halo_state,
    halo_documents,
    ext,
    conv,
    sconv,
    cum_rows,
    step_rows,
    in_rows,
    close_rows,
    weighted,
    part_ref,
    infl_ref,
    dep_ref,
    dep_stage,
    dep_in,
    fade_stage,
    fade_in,
    chain_out,
    chain_in,
    state_out,
    state_in,
    state_own,
    acts,
    partial,
    partial_own,
    sums_in,
    final_out,
    final_in,
    local_sems,
    halo_sems,
    weight_sems,
    pair_sems,
    chain_sems,
    state_sems,
    act_send,
    act_recv,
    sum_send,
    sum_recv,
    final_send,
    final_recv,
    weight_extra,
    extra_part,
    extra_own,
    extra_sums,
    extra_out,
    extra_weight_sems,
    extra_send,
    extra_recv,
    extra_final_send,
    extra_final_recv,
):
    s = lax.axis_index("seq")
    h = lax.axis_index("head")
    z, y = s // 2, s % 2
    me = s * 4 + h
    z_near = z + 1 - 2 * (z % 2)
    z_far = (z + 2) % 4
    y_pair = 2 * z + 1 - y
    z_pair = 2 * z_far + y

    def remote(src, dst, send, recv, seq, head=h):
        return pltpu.make_async_remote_copy(
            src_ref=src,
            dst_ref=dst,
            send_sem=send,
            recv_sem=recv,
            device_id=(seq, head),
            device_id_type=MESH,
        )

    gate_copy = pltpu.make_async_copy(gate_hbm, gate_ref, local_sems.at[0])
    weight_copy = pltpu.make_async_copy(weight_hbm, weight_ref, local_sems.at[1])
    gate_copy.start()
    weight_copy.start()

    barrier = pltpu.get_barrier_semaphore()

    @pl.loop(1, 32)
    def _(i):
        other = lax.rem(me + i, 32)
        pl.semaphore_signal(
            barrier, inc=1, device_id=(other // 4, other % 4), device_id_type=MESH
        )

    pl.semaphore_wait(barrier, 31)

    after = jnp.minimum(s + 1, 7)
    halo_copies = [
        remote(source, target, halo_sems.at[0, i], halo_sems.at[1, i], after)
        for i, (source, target) in enumerate(
            (
                (documents_ref, halo_documents),
                (state_ref.at[pl.ds(SPAN - 16, 16)], halo_state),
                (inner_ref.at[pl.ds(SPAN - 16, 16)], halo_inner),
            )
        )
    ]

    @pl.when(s < 7)
    def _():
        for copy in halo_copies:
            copy.start()

    def weight_parts(wide):
        parts = []
        for i in range(8):
            at = (pl.ds(i * 256, 256), pl.ds(0, wide))
            parts.append(
                remote(
                    weight_hbm.at[at],
                    weight_in.at[at],
                    weight_sems.at[0, i],
                    weight_sems.at[1, i],
                    2 * z_near + y,
                )
            )
        return parts

    weight_whole, weight_less = weight_parts(512), weight_parts(384)
    weight_aside = remote(
        weight_hbm.at[:, pl.ds(384, 128)],
        weight_extra,
        extra_weight_sems.at[0],
        extra_weight_sems.at[1],
        2 + y,
    )

    @pl.when(z == 2)
    def _():
        for copy in weight_less[:3]:
            copy.start()
        weight_aside.start()

    @pl.when(z == 0)
    def _():
        weight_whole[0].start()

    @pl.when(z % 2 == 1)
    def _():
        for copy in weight_whole:
            copy.start()

    @pl.when(z == 3)
    def _():
        weight_in[:, 384:512] = jnp.zeros((CHANNELS, 128), jnp.bfloat16)

    @pl.when(s == 0)
    def _():
        halo_documents[...] = jnp.zeros_like(halo_documents)
        halo_state[...] = jnp.zeros_like(halo_state)
        halo_inner[...] = jnp.zeros_like(halo_inner)

    diagonal = lax.broadcasted_iota(jnp.int32, (32, 32), 0) == lax.broadcasted_iota(
        jnp.int32, (32, 32), 1
    )
    rate = jnp.sum(
        jnp.where(diagonal, jnp.broadcast_to(jnp.exp(decay_ref[...]), (32, 32)), 0.0),
        axis=1,
        keepdims=True,
    )
    value = step_ref[...]
    step = jnp.maximum(value, 0.0) + jnp.log1p(jnp.exp(-jnp.abs(value)))
    row_at = lax.broadcasted_iota(jnp.int32, (SPAN, SPAN), 0)
    col_at = lax.broadcasted_iota(jnp.int32, (SPAN, SPAN), 1)
    upper = (row_at <= col_at).astype(jnp.float32)
    cumulative = jnp.dot(
        -step * rate, upper, precision=highest, preferred_element_type=jnp.float32
    )
    documents = documents_ref[...].astype(jnp.float32)
    final = (documents == documents[:, SPAN - 1 :]).astype(jnp.float32)
    step_rows[...] = step
    cum_rows[...] = cumulative
    close_rows[...] = jnp.exp(cumulative[:, SPAN - 1 :] - cumulative) * final * step

    @pl.when(s > 0)
    def _():
        for copy in halo_copies:
            copy.wait_recv()

    before = halo_documents[...].astype(jnp.float32)
    in_rows[...] = jnp.exp(cumulative) * (documents == before[:, SPAN - 1 :]).astype(jnp.float32)
    lane = lax.broadcasted_iota(jnp.int32, (8, SPAN), 1)
    mark_row = lax.broadcasted_iota(jnp.int32, (8, SPAN), 0)
    documents_8 = jnp.broadcast_to(documents, (8, SPAN))
    before_8 = jnp.broadcast_to(before, (8, SPAN))
    mark_rows = documents_8
    for k in (1, 2, 3):
        shifted = jnp.where(
            lane < k, pltpu.roll(before_8, k, axis=1), pltpu.roll(documents_8, k, axis=1)
        )
        same = (shifted == documents_8).astype(jnp.float32)
        mark_rows = jnp.where(mark_row == k, same, mark_rows)
    marks = mark_rows.T

    def convolve(source, halo, at, taps, target):
        lanes = pl.ds(at, 256)
        ext[0:16, :] = halo[:, lanes].astype(jnp.float32)
        ext[16:272, :] = source[:, lanes].astype(jnp.float32)
        running = marks[:, 3:4] * (ext[13:269, :] * taps(0, lanes))
        running = running + marks[:, 2:3] * (ext[14:270, :] * taps(1, lanes))
        running = running + marks[:, 1:2] * (ext[15:271, :] * taps(2, lanes))
        running = running + ext[16:272, :] * taps(3, lanes)
        target[:, lanes] = (running * jax.nn.sigmoid(running)).astype(jnp.bfloat16)

    for i in range(2):
        convolve(
            state_ref,
            halo_state,
            i * 256,
            lambda k, lanes, i=i: filter_state_ref[k, i : i + 1, :],
            sconv,
        )

    linked = (marks[:, 0:1] == documents) & (row_at >= col_at)
    low = lax.broadcasted_iota(jnp.int32, (SPAN, 128), 1) < HEAD_DIM

    apart = pl.ds(pl.multiple_of((1 - y) * HALF, HALF), HALF)
    send_dep = remote(dep_stage, dep_in, pair_sems.at[0], pair_sems.at[1], y_pair)
    send_fade = remote(fade_stage, fade_in, pair_sems.at[2], pair_sems.at[3], y_pair)

    @pl.loop(0, 2)
    def _(turn):
        group = jnp.where(turn == 0, 1 - y, y)
        base = group * HALF

        @pl.loop(0, 4)
        def _(i):
            at = pl.multiple_of(base + i * 256, 256)
            convolve(
                inner_ref,
                halo_inner,
                at,
                lambda k, lanes: filter_inner_ref[k : k + 1, lanes],
                conv,
            )

        writes = sconv[:, pl.ds(pl.multiple_of(group * 128, 128), 128)]
        heads = pl.ds(pl.multiple_of(group * 16, 16), 16)
        in_cols = in_rows[heads, :].T
        close_cols = close_rows[heads, :].T
        for pair in range(8):
            first = pair * 2
            at = pl.ds(pl.multiple_of(base + pair * 128, 128), 128)

            def both(cols):
                return jnp.where(low, cols[:, first : first + 1], cols[:, first + 1 : first + 2])

            weighted[:, pair * 128 : pair * 128 + 128] = (
                conv[:, at].astype(jnp.float32) * both(close_cols)
            ).astype(jnp.bfloat16)
            infl_ref[:, at] = both(in_cols)
        dep_ref[...] = lax.dot_general(
            writes, weighted[...], (((0,), (0,)), ((), ())), preferred_element_type=jnp.float32
        )

        @pl.when(turn == 0)
        def _():
            dep_stage[...] = dep_ref[...].astype(jnp.bfloat16)
            fade_stage[...] = infl_ref[SPAN - 8 : SPAN, apart]
            send_fade.start()
            send_dep.start()

    def mixing_of(group):
        base = group * HALF
        writes = sconv[:, pl.ds(pl.multiple_of(group * 128, 128), 128)]
        reads = sconv[:, pl.ds(pl.multiple_of(256 + group * 128, 128), 128)]
        scores = lax.dot_general(
            reads, writes, (((1,), (1,)), ((), ())), preferred_element_type=jnp.float32
        )
        scores = jnp.where(linked, scores, 0.0)
        heads = pl.ds(pl.multiple_of(group * 16, 16), 16)
        cums = cum_rows[heads, :]
        steps = step_rows[heads, :]
        cum_cols = cums.T
        for pair in range(8):
            first = pair * 2
            at = pl.ds(pl.multiple_of(base + pair * 128, 128), 128)
            x = conv[:, at]

            def mixed(j):
                spread = jnp.minimum(cum_cols[:, j : j + 1] - cums[j : j + 1, :], 0.0)
                mixing = (jnp.exp(spread) * scores * steps[j : j + 1, :]).astype(jnp.bfloat16)
                return jnp.dot(mixing, x, preferred_element_type=jnp.float32)

            gain = jnp.where(low, skip_ref[group * 16 + first], skip_ref[group * 16 + first + 1])
            part_ref[:, at] = jnp.where(low, mixed(first), mixed(first + 1)) + gain * x.astype(
                jnp.float32
            )

    @pl.when(z == 0)
    def _():
        chain_in[...] = jnp.zeros_like(chain_in)

    is_first = y == 0
    chain_copies = [
        remote(
            chain_out.at[q],
            chain_in.at[q],
            chain_sems.at[0, q],
            chain_sems.at[1, q],
            jnp.minimum(s + 2, 7),
        )
        for q in range(4)
    ]
    state_copies = [
        remote(state_out.at[q], state_in.at[q], state_sems.at[0, q], state_sems.at[1, q], y_pair)
        for q in range(4)
    ]
    def chain():
        send_fade.wait_recv()
        send_dep.wait_recv()
        for q in range(4):
            lanes = pl.ds(pl.multiple_of(y * HALF + q * 256, 256), 256)
            here = slice(q * 256, q * 256 + 256)
            dep_own = dep_ref[:, here]
            dep_other = dep_in[:, here].astype(jnp.float32)
            fade_own = infl_ref[SPAN - 8 : SPAN, lanes][7:8]
            fade_other = fade_in[7:8, here]
            dep_0 = jnp.where(is_first, dep_own, dep_other)
            dep_1 = jnp.where(is_first, dep_other, dep_own)
            fade_0 = jnp.where(is_first, fade_own, fade_other)
            fade_1 = jnp.where(is_first, fade_other, fade_own)
            slab = fade_1 * dep_0 + dep_1
            slab_fade = fade_0 * fade_1

            @pl.when(z > 0)
            def _():
                chain_copies[q].wait_recv()

            entering_0 = chain_in[q].astype(jnp.float32)
            chain_out[q] = (slab_fade * entering_0 + slab).astype(jnp.bfloat16)

            @pl.when(z < 3)
            def _():
                chain_copies[q].start()

            entering_1 = fade_0 * entering_0 + dep_0
            state_own[:, here] = jnp.where(is_first, entering_0, entering_1).astype(jnp.bfloat16)
            state_out[q] = jnp.where(is_first, entering_1, entering_0).astype(jnp.bfloat16)
            state_copies[q].start()

    @pl.loop(0, 3)
    def _(phase):
        late = jnp.where(z >= 2, 1, 0)

        @pl.when(phase != 1 + late)
        def _():
            mixing_of(jnp.where(phase == 0, 1 - y, y))

        @pl.when(phase == 1 + late)
        def _():
            chain()

    @pl.when(z == 0)
    def _():
        for copy in weight_whole[1:]:
            copy.start()

    @pl.when(z == 2)
    def _():
        for copy in weight_less[3:]:
            copy.start()

    gate_copy.wait()

    def act_copy(slot, half, quarter):
        source = 2 if slot == 3 else 0
        rows = pl.ds(quarter * 128, 128)
        return remote(
            acts.at[source, half, rows],
            acts.at[slot, half, rows],
            act_send.at[slot - 1, half, quarter],
            act_recv.at[slot - 1, half, quarter],
            z_pair if slot == 2 else y_pair,
        )

    def norm_half(half, state):
        lanes = pl.ds(pl.multiple_of(half * HALF, HALF), HALF)
        reads_at = pl.ds(pl.multiple_of(256 + half * 128, 128), 128)
        for quarter in range(2):

            @pl.loop(0, 2)
            def _(i):
                rows = pl.ds(pl.multiple_of(quarter * 128 + i * 64, 64), 64)
                read = jnp.dot(sconv[rows, reads_at], state, preferred_element_type=jnp.float32)
                gate = gate_ref[rows, lanes].astype(jnp.float32)
                scan = part_ref[rows, lanes] + infl_ref[rows, lanes] * read
                gated = scan * (gate * jax.nn.sigmoid(gate))
                mean = jnp.sum(gated * gated, axis=1, keepdims=True) * (1.0 / HALF)
                normed = gated * lax.rsqrt(mean + 1e-05) * gain_ref[:, lanes]
                acts[0, half, rows, :] = normed.astype(jnp.bfloat16)

            act_copy(2, half, quarter).start()
            act_copy(1, half, quarter).start()

    norm_half(y, state_own[...])
    for q in range(4):
        state_copies[q].wait_recv()
    norm_half(1 - y, jnp.concatenate([state_in[q] for q in range(4)], axis=1))

    def sum_copy(k, side, o):
        to = h ^ o
        rows = pl.ds(pl.multiple_of(to * 64, 64), 64)
        return remote(
            partial.at[k, side, rows],
            sums_in.at[k, side, o - 1],
            sum_send.at[k, side, o - 1],
            sum_recv.at[k, side, o - 1],
            s,
            to,
        )

    def project(k, side):
        weight = (weight_ref, weight_in)[side]

        @pl.loop(0, 2)
        def _(i):
            lanes = pl.ds(pl.multiple_of(i * 256, 256), 256)
            total = jnp.dot(
                acts[k, 0], weight[0:HALF, lanes], preferred_element_type=jnp.float32
            ) + jnp.dot(
                acts[k, 1], weight[HALF:CHANNELS, lanes], preferred_element_type=jnp.float32
            )
            partial_own[k, side, :, lanes] = total
            partial[k, side, :, lanes] = total.astype(jnp.bfloat16)

        for o in (2, 3, 1):
            sum_copy(k, side, o).start()

    rows_own = pl.ds(pl.multiple_of(h * 64, 64), 64)
    spot_own = pl.ds(pl.multiple_of(y * 512, 512), 512)

    def final_target(k):
        return 2 * (z if k < 2 else z_far) + (y if k % 2 == 0 else 1 - y)

    def final_part(k, side, wide):
        spot = pl.ds(pl.multiple_of(y * 512, 512), wide)
        return remote(
            final_out.at[k, side, :, pl.ds(0, wide)],
            final_in.at[rows_own, spot],
            final_send.at[k, side],
            final_recv.at[y * 4 + h],
            final_target(k),
            z if side == 0 else z_near,
        )

    def final_cases(k, side):
        head = z if side == 0 else z_near
        leaves = head != h if k == 0 else head >= 0
        if side == 0:
            return [(leaves, 512)]
        return [(leaves & (z < 3), 512), (leaves & (z == 3), 384)]

    def finish(k, side):
        for o in (1, 2, 3):
            sum_copy(k, side, o).wait_recv()
        total = partial_own[k, side, rows_own, :]
        for o in range(3):
            total = total + sums_in[k, side, o].astype(jnp.float32)
        final_out[k, side] = total.astype(jnp.bfloat16)
        for case, wide in final_cases(k, side):

            @pl.when(case)
            def _():
                final_part(k, side, wide).start()

        if k == 0:
            stays = (z if side == 0 else z_near) == h
            less = (z == 3) & (side == 1)

            @pl.when(stays & jnp.logical_not(less))
            def _():
                final_in[rows_own, spot_own] = final_out[k, side]

            @pl.when(stays & less)
            def _():
                spot = pl.ds(pl.multiple_of(y * 512, 512), 384)
                final_in[rows_own, spot] = final_out[k, side, :, 0:384]

    spot_extra = pl.ds(pl.multiple_of(y * 512 + 384, 128), 128)

    def extra_copy(k, o):
        to = h ^ o
        return remote(
            extra_part.at[k, pl.ds(pl.multiple_of(to * 64, 64), 64)],
            extra_sums.at[k, o - 1],
            extra_send.at[k, o - 1],
            extra_recv.at[k, o - 1],
            s,
            to,
        )

    def project_extra(k):
        total = jnp.dot(
            acts[k, 0], weight_extra[0:HALF, :], preferred_element_type=jnp.float32
        ) + jnp.dot(
            acts[k, 1], weight_extra[HALF:CHANNELS, :], preferred_element_type=jnp.float32
        )
        extra_own[k] = total
        extra_part[k] = total.astype(jnp.bfloat16)
        for o in (2, 3, 1):
            extra_copy(k, o).start()

    def extra_final(k):
        return remote(
            extra_out.at[k],
            final_in.at[rows_own, spot_extra],
            extra_final_send.at[k],
            extra_final_recv.at[y * 4 + h],
            final_target(k),
            2,
        )

    def finish_extra(k):
        for o in (1, 2, 3):
            extra_copy(k, o).wait_recv()
        total = extra_own[k, rows_own, :]
        for o in range(3):
            total = total + extra_sums[k, o].astype(jnp.float32)
        extra_out[k] = total.astype(jnp.bfloat16)
        if k > 0:
            extra_final(k).start()
            return

        @pl.when(h != 2)
        def _():
            extra_final(k).start()

        @pl.when(h == 2)
        def _():
            final_in[rows_own, spot_extra] = extra_out[k]

    def arrived(slot, half):
        for quarter in range(2):
            act_copy(slot, half, quarter).wait_recv()
            if slot == 2:
                act_copy(3, half, quarter).start()

    weight_copy.wait()
    project(0, 0)
    arrived(1, 1 - y)
    arrived(1, y)
    project(1, 0)
    finish(0, 0)
    arrived(2, y)
    finish(1, 0)

    def first_blocks(copies):
        for copy in copies:
            copy.wait_recv()
        project(0, 1)
        project(1, 1)
        finish(0, 1)

    @pl.when(z < 3)
    def _():
        first_blocks(weight_whole)

    @pl.when(z == 1)
    def _():
        weight_aside.wait_recv()
        project_extra(0)
        project_extra(1)

    arrived(2, 1 - y)
    project(2, 0)

    @pl.when(z < 3)
    def _():
        finish(1, 1)

    finish(2, 0)

    @pl.when(z == 3)
    def _():
        first_blocks(weight_less)
        finish(1, 1)

    project(2, 1)

    @pl.when(z == 1)
    def _():
        project_extra(2)
        finish_extra(0)
        finish_extra(1)

    arrived(3, 1 - y)
    arrived(3, y)
    project(3, 0)
    finish(2, 1)
    project(3, 1)

    @pl.when(z == 1)
    def _():
        project_extra(3)
        finish_extra(2)

    finish(3, 0)
    finish(3, 1)

    @pl.when(z == 1)
    def _():
        finish_extra(3)


    z_from = 2 * (h // 2) + z % 2
    for y_from in range(2):
        for h_from in range(4):
            rows = slice(h_from * 64, h_from * 64 + 64)
            spot = slice(y_from * 512, y_from * 512 + 512)
            here = (y_from == y) & (h_from == h)
            remote_piece = jnp.logical_not((z_from == z) & here)
            less = (z % 2 == 1) & (h == 2)

            def piece(source, columns, sems):
                return remote(
                    source,
                    final_in.at[rows, columns],
                    final_send.at[0, 0],
                    sems.at[y_from * 4 + h_from],
                    2 * z_from + y_from,
                    h_from,
                )

            @pl.when(remote_piece & jnp.logical_not(less))
            def _():
                piece(final_out.at[0, 0], spot, final_recv).wait_recv()

            @pl.when(remote_piece & less)
            def _():
                columns = slice(y_from * 512, y_from * 512 + 384)
                piece(final_out.at[0, 0, :, pl.ds(0, 384)], columns, final_recv).wait_recv()

            @pl.when(less & jnp.logical_not((z == 1) & here))
            def _():
                columns = slice(y_from * 512 + 384, y_from * 512 + 512)
                piece(extra_out.at[0], columns, extra_final_recv).wait_recv()

    out_ref[...] = final_in[...]

    @pl.when(s < 7)
    def _():
        for copy in halo_copies:
            copy.wait_send()

    send_dep.wait_send()
    send_fade.wait_send()
    @pl.when(z == 2)
    def _():
        for copy in weight_less:
            copy.wait_send()
        weight_aside.wait_send()

    @pl.when(z != 2)
    def _():
        for copy in weight_whole:
            copy.wait_send()

    for q in range(4):
        state_copies[q].wait_send()

        @pl.when(z < 3)
        def _():
            chain_copies[q].wait_send()

    for slot in (1, 2, 3):
        for half in range(2):
            for quarter in range(2):
                act_copy(slot, half, quarter).wait_send()
    for k in range(4):
        for side in range(2):
            for o in (1, 2, 3):
                sum_copy(k, side, o).wait_send()
            for case, wide in final_cases(k, side):

                @pl.when(case)
                def _():
                    final_part(k, side, wide).wait_send()

    @pl.when(z == 1)
    def _():
        for k in range(4):
            for o in (1, 2, 3):
                extra_copy(k, o).wait_send()

            @pl.when((h != 2) if k == 0 else (h >= 0))
            def _():
                extra_final(k).wait_send()


def on_device_fast(
    inner_input,
    state_input,
    gate_input,
    step_input,
    decay_exponent,
    skip_gain,
    documents,
    filter_inner,
    filter_state,
    norm_gain,
    output_weight,
):
    vmem = pl.BlockSpec(memory_space=pltpu.VMEM)
    smem = pl.BlockSpec(memory_space=pltpu.SMEM)
    anywhere = pl.BlockSpec(memory_space=pl.ANY)
    bf16, f32 = jnp.bfloat16, jnp.float32
    dma = pltpu.SemaphoreType.DMA
    return pl.pallas_call(
        fused_kernel,
        out_shape=jax.ShapeDtypeStruct((SPAN, 1024), bf16),
        in_specs=[vmem] * 8 + [smem] + [anywhere] * 2,
        out_specs=vmem,
        scratch_shapes=[
            pltpu.VMEM((SPAN, CHANNELS), bf16),
            pltpu.VMEM((CHANNELS, 512), bf16),
            pltpu.VMEM((CHANNELS, 512), bf16),
            pltpu.VMEM((16, CHANNELS), bf16),
            pltpu.VMEM((16, 512), bf16),
            pltpu.VMEM((1, SPAN), jnp.int32),
            pltpu.VMEM((SPAN + 16, 256), f32),
            pltpu.VMEM((SPAN, CHANNELS), bf16),
            pltpu.VMEM((SPAN, 512), bf16),
            pltpu.VMEM((32, SPAN), f32),
            pltpu.VMEM((32, SPAN), f32),
            pltpu.VMEM((32, SPAN), f32),
            pltpu.VMEM((32, SPAN), f32),
            pltpu.VMEM((SPAN, HALF), bf16),
            pltpu.VMEM((SPAN, CHANNELS), f32),
            pltpu.VMEM((SPAN, CHANNELS), f32),
            pltpu.VMEM((STATE, HALF), f32),
            pltpu.VMEM((STATE, HALF), bf16),
            pltpu.VMEM((STATE, HALF), bf16),
            pltpu.VMEM((8, HALF), f32),
            pltpu.VMEM((8, HALF), f32),
            pltpu.VMEM((4, STATE, 256), bf16),
            pltpu.VMEM((4, STATE, 256), bf16),
            pltpu.VMEM((4, STATE, 256), bf16),
            pltpu.VMEM((4, STATE, 256), bf16),
            pltpu.VMEM((STATE, HALF), bf16),
            pltpu.VMEM((4, 2, SPAN, HALF), bf16),
            pltpu.VMEM((4, 2, SPAN, 512), bf16),
            pltpu.VMEM((4, 2, SPAN, 512), f32),
            pltpu.VMEM((4, 2, 3, 64, 512), bf16),
            pltpu.VMEM((4, 2, 64, 512), bf16),
            pltpu.VMEM((SPAN, 1024), bf16),
            dma((2,)),
            dma((2, 3)),
            dma((2, 8)),
            dma((4,)),
            dma((2, 4)),
            dma((2, 4)),
            dma((3, 2, 2)),
            dma((3, 2, 2)),
            dma((4, 2, 3)),
            dma((4, 2, 3)),
            dma((4, 2)),
            dma((8,)),
            pltpu.VMEM((CHANNELS, 128), bf16),
            pltpu.VMEM((4, SPAN, 128), bf16),
            pltpu.VMEM((4, SPAN, 128), f32),
            pltpu.VMEM((4, 3, 64, 128), bf16),
            pltpu.VMEM((4, 64, 128), bf16),
            dma((2,)),
            dma((4, 3)),
            dma((4, 3)),
            dma((4,)),
            dma((8,)),
        ],
        compiler_params=pltpu.CompilerParams(
            vmem_limit_bytes=56 * MIB, collective_id=0, has_side_effects=True
        ),
        name="layer",
    )(
        inner_input,
        state_input.reshape(SPAN, 512),
        step_input,
        decay_exponent[None, :],
        documents[None, :],
        filter_inner,
        filter_state,
        norm_gain[None, :],
        skip_gain,
        gate_input,
        output_weight,
    )


def solution(mesh):
    placed = (
        P("seq", "head"),
        P("seq", None, "head"),
        P("seq", "head"),
        P("head", "seq"),
        P("head"),
        P("head"),
        P("seq"),
        P(None, "head"),
        P(None, None, "head"),
        P("head"),
        P("head", "seq"),
    )
    ways = dict(mesh.shape)
    fast = ways["seq"] == 8 and ways["head"] == 4
    return jax.shard_map(
        on_device_fast if fast else on_device, mesh=mesh, in_specs=placed, out_specs=P("seq", "head"), check_vma=False
    )
```
